256 devices in a mesh: seq: 64 (over z, x, core), tp: 4 (over y).
Axes of the slice: x: 4, y: 4, z: 8, core: 2. Of those that a mesh axis runs over, the one named last changes fastest.
Arguments:
- queries: bfloat16 [16384, 4096], P('seq', 'tp'), may hold values from -16 to 16
- key_states: bfloat16 [16384, 1024], P('seq', 'tp'), may hold values from -4 to 4
- value_states: bfloat16 [16384, 1024], P('seq', 'tp'), may hold values from -4 to 4
- vert_blocks: int32 [32, 16], P('tp'), may hold values from 0 to 127, as said below
- window_size: int32 [32], P('tp'), may hold values from 1 to 64
- slash_offsets: int32 [32, 8], P('tp'), may hold values from 1 to 128, as said below
- out_weight: bfloat16 [4096, 4096], P('tp'), may hold values from -0.59765625 to 0.59765625
Outputs:
- mixed: bfloat16 [16384, 4096], P('seq', 'tp')
The draws below stay inside these ranges and needn't reach their ends.
Inputs may be any that keep to these rules, and one draw needn't show every extreme that they name: `vert_blocks`: each row names 16 distinct blocks. For each key head, the blocks named by its 4 query heads include at most 1 of the 2 blocks of one index of seq, and exactly 1 for some index. `slash_offsets`: each head's 8 offsets are distinct and no smaller than that head's window_size.
All inputs are finite; a program needn't handle non-finite values.
Results may differ from the reference program's by a relative error of at most 0.0055.
Values may be sent and summed in bfloat16 or wider, within the bound.
No kernel may reach another device: no remote copies, remote signals or barrier semaphores. Data moves between devices by JAX's collectives and lax.ppermute only.
A program may use at most 128 MiB of HBM per device.

```python
import math
import jax
import jax.numpy as jnp
from jax import lax

H = 32
KVH = 8
HD = 128
D = 4096
TOK_DEV = 256
BLK = 128
NV = 16
NS = 8
GROUP = 4
SEQ_LEN = 16384
NB = 2
NBLK = 128
CAPV = 1
N_SEQ = 64


def window_of(key):
    picked = jax.random.randint(key, (H,), 1, TOK_DEV // 4 + 1, dtype=jnp.int32)
    return picked.at[0].set(TOK_DEV // 4).at[1].set(1)


def draw_queries(key, part):
    key = jax.random.fold_in(key, 7)
    return jnp.clip(jax.random.normal(key, (SEQ_LEN, H * HD), jnp.float32), -4.0, 4.0).astype(jnp.bfloat16)


def draw_key_states(key, part):
    key = jax.random.fold_in(key, 3)
    return jnp.clip(jax.random.normal(key, (SEQ_LEN, KVH * HD), jnp.float32), -4.0, 4.0).astype(jnp.bfloat16)


def union_of(group_key, shard_total):
    score_key, within_key = jax.random.split(group_key, 2)
    later_ids = jnp.arange(1, N_SEQ, dtype=jnp.int32)
    rough = jax.random.randint(score_key, (N_SEQ - 1,), 0, N_SEQ, dtype=jnp.int32) + later_ids
    distinct = rough * N_SEQ + later_ids
    picked = lax.top_k(distinct, shard_total - 1)[1].astype(jnp.int32) + 1
    shards = jnp.concatenate([jnp.zeros((1,), jnp.int32), picked])
    within_keys = jax.random.split(within_key, shard_total)
    within = jax.vmap(lambda one_key: jax.random.permutation(one_key, NB)[:CAPV])(within_keys).astype(jnp.int32)
    return (within + shards[:, None] * NB).reshape(-1)


def draw_vert_blocks(key, part):
    key = jax.random.fold_in(key, 11)
    owner_seed, pick_seed = jax.random.split(key, 2)
    shard_total = min(N_SEQ, max(1, (GROUP * NV + CAPV - 1) // CAPV))
    pool_size = shard_total * CAPV
    group_keys = jax.random.split(owner_seed, KVH)
    order_keys = jax.random.split(pick_seed, KVH)
    head_rows = []
    for group_id in range(KVH):
        union_blocks = union_of(group_keys[group_id], shard_total)
        pool_order = jax.random.permutation(order_keys[group_id], pool_size).astype(jnp.int32)
        for member in range(GROUP):
            positions = (member * NV + jnp.arange(NV, dtype=jnp.int32)) % pool_size
            head_rows.append(union_blocks[pool_order[positions]])
    return jnp.stack(head_rows).astype(jnp.int32)


def draw_window_size(key, part):
    shared = window_of(key)
    return shared


def draw_slash_offsets(key, part):
    shared = window_of(key)
    key = jax.random.fold_in(key, 9)
    offset_range = TOK_DEV // 4 + 1
    head_keys = jax.random.split(key, H)
    extras = jax.vmap(lambda head_key: jax.random.permutation(head_key, offset_range)[:NS])(head_keys).astype(jnp.int32)
    extras = extras.at[0].set(TOK_DEV // 4 - jnp.arange(NS, dtype=jnp.int32)).at[1].set(jnp.arange(NS, dtype=jnp.int32))
    return (shared[:, None] + extras).astype(jnp.int32)


def level_of(key, dims, pieces, low, high):
    def one(axis_at, blocks):
        heights = jax.random.uniform(jax.random.fold_in(jax.random.fold_in(key, 6), axis_at), (blocks,), jnp.float32, low / len(pieces), high / len(pieces))
        return jnp.repeat(jnp.exp(heights), dims[axis_at] // blocks).reshape((-1,) + (1,) * (len(dims) - axis_at - 1))

    factor_of = one(*pieces[0])
    for cut in pieces[1:]:
        factor_of = factor_of * one(*cut)
    return factor_of


def centred(stream_key, shape, scale, bound, cuts=(), kind=jnp.bfloat16):
    result = scale * jax.random.normal(stream_key, shape, jnp.float32)
    if cuts:
        result = result * level_of(stream_key, shape, cuts, -0.22, 0.18)
    return jnp.clip(result, -bound, bound).astype(kind)


def setup_inputs(seed: int = 0) -> dict:
    arg_keys = jax.random.split(jax.random.key(seed), 8)
    return {
        "queries": draw_queries(jax.random.fold_in(arg_keys[7], 71), 0),
        "key_states": draw_key_states(jax.random.fold_in(arg_keys[7], 71), 0),
        "value_states": centred(arg_keys[2], (SEQ_LEN, KVH * HD), 1.0, 4.0, ((0, 64), (1, 4))),
        "vert_blocks": draw_vert_blocks(jax.random.fold_in(arg_keys[7], 71), 0),
        "window_size": draw_window_size(jax.random.fold_in(arg_keys[7], 71), 0),
        "slash_offsets": draw_slash_offsets(jax.random.fold_in(arg_keys[7], 71), 0),
        "out_weight": centred(arg_keys[6], (H * HD, D), 0.1, 0.59765625, ((0, 4),)),
    }


NEG_FILL = -1e+30

def slash_match(gap, slash_offsets):
    slash_mask = gap == slash_offsets[:, 0][:, None, None]
    for column in range(1, slash_offsets.shape[1]):
        slash_mask = slash_mask | (gap == slash_offsets[:, column][:, None, None])
    return slash_mask

def attend_context(query_rows, local_keys, local_values, vert_keys, vert_values, vert_blocks, window_size, slash_offsets, start_row):
    row_count = query_rows.shape[0]
    head_count = vert_blocks.shape[0]
    kv_heads = local_keys.shape[1]
    group_size = head_count // kv_heads
    head_dim = local_keys.shape[2]
    key_span = local_keys.shape[0]
    score_scale = 1.0 / math.sqrt(head_dim)
    grouped = query_rows.reshape(row_count, kv_heads, group_size, head_dim)
    local_scores = jnp.einsum('sgeh,tgh->gest', grouped, local_keys, preferred_element_type=jnp.float32).reshape(head_count, row_count, key_span) * score_scale
    per_head = query_rows.reshape(row_count, head_count, head_dim).transpose(1, 0, 2)
    vert_scores = jnp.einsum('hsd,hkd->hsk', per_head, vert_keys, preferred_element_type=jnp.float32) * score_scale
    query_pos = start_row + jnp.arange(row_count, dtype=jnp.int32)
    local_pos = start_row - (key_span - row_count) + jnp.arange(key_span, dtype=jnp.int32)
    local_gap = (query_pos[:, None] - local_pos[None, :])[None]
    window_col = window_size[:, None, None]
    local_ok = (local_pos[None, None, :] >= 0) & ((local_gap >= 0) & (local_gap < window_col) | slash_match(local_gap, slash_offsets))
    block_rows = vert_keys.shape[1] // vert_blocks.shape[1]
    vert_pos = (vert_blocks[:, :, None] * block_rows + jnp.arange(block_rows, dtype=jnp.int32)[None, None, :]).reshape(head_count, -1)
    vert_gap = query_pos[None, :, None] - vert_pos[:, None, :]
    vert_ok = (vert_gap >= window_col) & jnp.logical_not(slash_match(vert_gap, slash_offsets))
    local_scores = jnp.where(local_ok, local_scores, NEG_FILL)
    vert_scores = jnp.where(vert_ok, vert_scores, NEG_FILL)
    row_max = jnp.maximum(lax.optimization_barrier(jnp.max(local_scores, axis=2)), lax.optimization_barrier(jnp.max(vert_scores, axis=2)))[:, :, None]
    local_weights = jnp.where(local_ok, jnp.exp(local_scores - row_max), 0.0)
    vert_weights = jnp.where(vert_ok, jnp.exp(vert_scores - row_max), 0.0)
    denominator = lax.optimization_barrier(jnp.sum(local_weights, axis=2)) + lax.optimization_barrier(jnp.sum(vert_weights, axis=2))
    local_part = jnp.einsum('gest,tgh->gesh', local_weights.astype(jnp.bfloat16).reshape(kv_heads, group_size, row_count, key_span), local_values, preferred_element_type=jnp.float32).reshape(head_count, row_count, head_dim)
    vert_part = jnp.einsum('hsk,hkd->hsd', vert_weights.astype(jnp.bfloat16), vert_values, preferred_element_type=jnp.float32)
    context = (local_part + vert_part) / denominator[:, :, None]
    return context.transpose(1, 0, 2).reshape(row_count, head_count * head_dim).astype(jnp.bfloat16)

def reference(queries, key_states, value_states, vert_blocks, window_size, slash_offsets, out_weight):
    half_rows = TOK_DEV // 2
    head_group = jnp.arange(H, dtype=jnp.int32) // GROUP
    key_blocks = key_states.reshape(NBLK, BLK, KVH, HD)
    value_blocks = value_states.reshape(NBLK, BLK, KVH, HD)
    vert_keys = key_blocks[vert_blocks, :, head_group[:, None], :].reshape(H, NV * BLK, HD)
    vert_values = value_blocks[vert_blocks, :, head_group[:, None], :].reshape(H, NV * BLK, HD)
    padded_keys = jnp.concatenate([jnp.zeros((half_rows, KVH * HD), key_states.dtype), key_states], axis=0)
    padded_values = jnp.concatenate([jnp.zeros((half_rows, KVH * HD), value_states.dtype), value_states], axis=0)

    def one_shard(shard_index):
        start_row = (shard_index * TOK_DEV).astype(jnp.int32)
        query_rows = lax.dynamic_slice_in_dim(queries, start_row, TOK_DEV, 0)
        local_keys = lax.dynamic_slice_in_dim(padded_keys, start_row, half_rows + TOK_DEV, 0).reshape(half_rows + TOK_DEV, KVH, HD)
        local_values = lax.dynamic_slice_in_dim(padded_values, start_row, half_rows + TOK_DEV, 0).reshape(half_rows + TOK_DEV, KVH, HD)
        return attend_context(query_rows, local_keys, local_values, vert_keys, vert_values, vert_blocks, window_size, slash_offsets, start_row)
    contexts = lax.map(one_shard, jnp.arange(N_SEQ, dtype=jnp.int32))
    context = contexts.reshape(SEQ_LEN, H * HD)
    return jnp.dot(context, out_weight, preferred_element_type=jnp.float32).astype(jnp.bfloat16)
```

```python
import functools
import math

import jax
import jax.numpy as jnp
from jax import lax
from jax.experimental import pallas as pl
from jax.experimental.pallas import tpu as pltpu
from jax.sharding import PartitionSpec as P

HD = 128
BLK = 128
GROUP = 4
NX, NZ = 4, 8
NEG = -1e30
C2 = math.log2(math.e) / math.sqrt(HD)
VMEM_BYTES = 48 * 1024 * 1024


def seq_at(z, x, core):
    return ((z % NZ) * NX + (x % NX)) * 2 + core


def shift(value, dz, dx, flip=0):
    pairs = [
        (seq_at(z, x, c), seq_at(z + dz, x + dx, c ^ flip))
        for z in range(NZ)
        for x in range(NX)
        for c in range(2)
    ]
    return lax.ppermute(value, "seq", pairs)


def tp_shift(value, step):
    return lax.ppermute(value, "tp", [(i, (i + step) % 4) for i in range(4)])


def dot_t(a, b, dims):
    return lax.dot_general(a, b, (dims, ((), ())), preferred_element_type=jnp.float32)


def local_kernel(scal, win, slash, named, q_ref, kv_ref, halo_ref, m_ref, l_ref, acc_ref):
    has_prev = scal[0] > 0
    kj = lax.broadcasted_iota(jnp.int32, (BLK, BLK), 0)
    qi = lax.broadcasted_iota(jnp.int32, (BLK, BLK), 1)
    diag_gap = qi - kj
    prev_gap = diag_gap + BLK
    keys = jnp.concatenate([halo_ref[:, :HD], kv_ref[:, :HD]], axis=0)
    values = jnp.concatenate([halo_ref[:, HD:], kv_ref[:, HD:]], axis=0)
    for h in range(GROUP):
        diag_ok = diag_gap < win[h]
        prev_ok = prev_gap < win[h]
        for n in range(8):
            diag_ok = diag_ok | (diag_gap == slash[h, n])
            prev_ok = prev_ok | (prev_gap == slash[h, n])
        for i in range(4):
            span = (i + 2) * BLK
            s = dot_t(keys[:span], q_ref[h, i * BLK : (i + 1) * BLK, :], ((1,), (1,)))
            tiles = []
            for t in range(i + 2):
                tile = s[t * BLK : (t + 1) * BLK]
                is_named = named[h, t] > 0
                if t == i + 1:
                    ok = (diag_gap >= 0) & (diag_ok | is_named)
                elif t == i:
                    ok = prev_ok | is_named
                    if t == 0:
                        ok = ok & has_prev
                else:
                    ok = jnp.broadcast_to(is_named, (BLK, BLK))
                tiles.append(jnp.where(ok, tile, NEG))
            s = jnp.concatenate(tiles, axis=0)
            m = jnp.max(s, axis=0, keepdims=True)
            w = jnp.exp2((s - m) * C2)
            m_ref[h, :, i * BLK : (i + 1) * BLK] = m
            l_ref[h, :, i * BLK : (i + 1) * BLK] = jnp.sum(w, axis=0, keepdims=True)
            acc_ref[h, :, i * BLK : (i + 1) * BLK] = dot_t(
                values[:span], w.astype(jnp.bfloat16), ((0,), (0,))
            )


def far_kernel(first, sizes, final, act, q_ref, m_in, l_in, acc_in, *rest):
    pieces = rest[: len(sizes)]
    if final:
        out_ref, m_ref, l_ref, acc_ref, kv, todo, sem = rest[len(sizes) :]
    else:
        m_ref, l_ref, acc_ref, kv, todo, sem = rest[len(sizes) :]
    copies = []
    at = 0
    for k, (piece, size) in enumerate(zip(pieces, sizes)):
        copies.append(pltpu.make_async_copy(piece, kv.at[pl.ds(at, size)], sem.at[k]))
        at += size
    for copy in copies:
        copy.start()

    def note(k, count):
        slot = k // GROUP
        todo[count] = k
        return count + act[k - slot * GROUP, first + slot]

    count = lax.fori_loop(0, at * GROUP, note, 0)
    m_ref[...] = m_in[...]
    l_ref[...] = l_in[...]
    acc_ref[...] = acc_in[...]
    for copy in copies:
        copy.wait()

    def scores(k):
        slot = k // GROUP
        h = k - slot * GROUP
        return slot, h, dot_t(kv[slot, :, :HD], q_ref[h], ((1,), (1,)))

    def merge(slot, h, s):
        m_old = m_ref[h]
        m_new = jnp.maximum(m_old, jnp.max(s, axis=0, keepdims=True))
        alpha = jnp.exp2((m_old - m_new) * C2)
        w = jnp.exp2((s - m_new) * C2)
        m_ref[h] = m_new
        l_ref[h] = l_ref[h] * alpha + jnp.sum(w, axis=0, keepdims=True)
        acc_ref[h] = acc_ref[h] * alpha + dot_t(
            kv[slot, :, HD:], w.astype(jnp.bfloat16), ((0,), (0,))
        )

    def two(k, carry):
        one = scores(todo[2 * k])
        other = scores(todo[2 * k + 1])
        merge(*one)
        merge(*other)
        return carry

    lax.fori_loop(0, count // 2, two, 0)

    @pl.when(count % 2 == 1)
    def _():
        merge(*scores(todo[count - 1]))

    if final:
        for h in range(GROUP):
            done = acc_ref[h] / l_ref[h]
            out_ref[:, h * HD : (h + 1) * HD] = done.T.astype(jnp.bfloat16)


def spec(space):
    return pl.BlockSpec(memory_space=space)


def state_shapes(rows):
    return [
        jax.ShapeDtypeStruct((GROUP, 1, rows), jnp.float32),
        jax.ShapeDtypeStruct((GROUP, 1, rows), jnp.float32),
        jax.ShapeDtypeStruct((GROUP, HD, rows), jnp.float32),
    ]


def attend_local(scal, win, slash, named, q4, kv, halo):
    rows = kv.shape[0]
    return pl.pallas_call(
        local_kernel,
        out_shape=state_shapes(rows),
        in_specs=[spec(pltpu.SMEM)] * 4 + [spec(pltpu.VMEM)] * 3,
        out_specs=[spec(pltpu.VMEM)] * 3,
        compiler_params=pltpu.CompilerParams(vmem_limit_bytes=VMEM_BYTES),
        cost_estimate=pl.CostEstimate(flops=500_000_000, bytes_accessed=4_000_000, transcendentals=0),
        name="local_part",
    )(scal, win, slash, named, q4, kv, halo)


def attend_far(act, q4, state, pieces, first, final):
    rows = q4.shape[1]
    sizes = [p.shape[0] for p in pieces]
    total = sum(sizes)
    outs = state_shapes(rows)
    scratch = [
        pltpu.VMEM((total, BLK, 2 * HD), jnp.bfloat16),
        pltpu.SMEM((total * GROUP + 8,), jnp.int32),
        pltpu.SemaphoreType.DMA((len(sizes),)),
    ]
    if final:
        scratch = [pltpu.VMEM(o.shape, o.dtype) for o in outs] + scratch
        outs = [jax.ShapeDtypeStruct((rows, GROUP * HD), jnp.bfloat16)]
    return pl.pallas_call(
        functools.partial(far_kernel, first, sizes, final),
        out_shape=outs,
        in_specs=[spec(pltpu.SMEM)] + [spec(pltpu.VMEM)] * 4 + [spec(pl.ANY)] * len(sizes),
        out_specs=[spec(pltpu.VMEM)] * len(outs),
        scratch_shapes=scratch,
        compiler_params=pltpu.CompilerParams(vmem_limit_bytes=VMEM_BYTES),
        cost_estimate=pl.CostEstimate(
            flops=total * 30_000_000, bytes_accessed=4_000_000, transcendentals=0
        ),
        name="far_part",
    )(act, q4, *state, *pieces)


def local(queries, key_states, value_states, vert_blocks, window_size, slash_offsets, out_weight):
    place = lax.axis_index("seq")
    core = place % 2
    chip = place // 2
    z, x = chip // NX, chip % NX
    first_core = core == 0

    def mine_other(a, axis):
        half = a.shape[axis] // 2
        low = lax.slice_in_dim(a, 0, half, axis=axis)
        high = lax.slice_in_dim(a, half, 2 * half, axis=axis)
        return jnp.where(first_core, low, high), jnp.where(first_core, high, low)

    k_mine, k_other = mine_other(key_states, 1)
    v_mine, v_other = mine_other(value_states, 1)
    q_mine, q_other = mine_other(queries, 1)
    blocks = mine_other(vert_blocks, 0)[0]
    window = mine_other(window_size, 0)[0]
    slashes = mine_other(slash_offsets, 0)[0]

    kv_mine = jnp.concatenate([k_mine, v_mine], axis=1)
    kv_sib = shift(jnp.concatenate([k_other, v_other], axis=1), 0, 0, 1)
    q_sib = shift(q_other, 0, 0, 1)

    def chosen(kv, shard):
        second = jnp.any(blocks == 2 * shard + 1)
        return jnp.where(second, kv[BLK:], kv[:BLK])[None]

    a0 = chosen(kv_mine, place)
    b0 = chosen(kv_sib, place + 1 - 2 * core)

    a = jnp.concatenate([a0, shift(a0, 0, 1), shift(a0, 0, -1), shift(a0, 0, 2)], axis=0)
    ups, downs = [a], [a]
    for _ in range(3):
        ups.append(shift(ups[-1], 1, 0))
        downs.append(shift(downs[-1], -1, 0))
    up4 = shift(ups[3][:2], 1, 0)
    down4 = shift(downs[3][2:], -1, 0)

    bu, bd = [b0], [b0]
    for _ in range(3):
        bu.append(shift(bu[-1], 1, 0))
        bd.append(shift(bd[-1], -1, 0))
    bu4 = shift(bu[3], 1, 0)
    b = jnp.concatenate(bu + [bu4] + bd[1:], axis=0)
    b_right = shift(b, 0, 1)
    b_left = shift(b, 0, -1)
    b_right2 = shift(b_right[:4], 0, 1)
    b_left2 = shift(b_left[4:], 0, -1)

    ax = [0, -1, 1, 2]
    bz = [0, -1, -2, -3, -4, 1, 2, 3]

    def a_slots(dz, xs=ax):
        return [(dz, dx, 0) for dx in xs]

    def b_slots(dx, zs=bz):
        return [(dz, dx, 1) for dz in zs]

    groups = [
        ([a, ups[1], downs[1], b], a_slots(0) + a_slots(-1) + a_slots(1) + b_slots(0)),
        (
            [ups[2], downs[2], ups[3], downs[3], b_right, b_left],
            a_slots(-2) + a_slots(2) + a_slots(-3) + a_slots(3) + b_slots(-1) + b_slots(1),
        ),
        (
            [up4, down4, b_right2, b_left2],
            a_slots(-4, ax[:2]) + a_slots(4, ax[2:]) + b_slots(-2, bz[:4]) + b_slots(2, bz[4:]),
        ),
    ]
    slots = jnp.array([s for _, ss in groups for s in ss], dtype=jnp.int32)
    slot_z = (z + slots[:, 0] + NZ) % NZ
    slot_x = (x + slots[:, 1] + NX) % NX
    slot_core = jnp.where(slots[:, 2] == 0, core, 1 - core)
    slot_shard = (slot_z * NX + slot_x) * 2 + slot_core
    far = blocks <= 4 * chip - 2
    act = jnp.any(
        (blocks[:, :, None] // 2 == slot_shard[None, None, :]) & far[:, :, None], axis=1
    ).astype(jnp.int32)
    near = 4 * chip - 1 + jnp.arange(5, dtype=jnp.int32)
    named = jnp.any(blocks[:, :, None] == near[None, None, :], axis=1).astype(jnp.int32)

    def in_order(mine, sib):
        return jnp.where(
            first_core, jnp.concatenate([mine, sib], axis=0), jnp.concatenate([sib, mine], axis=0)
        )

    kv_chip = in_order(kv_mine, kv_sib)
    tail = jnp.where(first_core, kv_sib[BLK:], kv_mine[BLK:])
    halo = lax.ppermute(tail, "seq", [(i, i + 2) for i in range(2 * NX * NZ - 2)])
    q_chip = in_order(q_mine, q_sib)
    q4 = jnp.stack([q_chip[:, h * HD : (h + 1) * HD] for h in range(GROUP)], axis=0)

    state = attend_local(chip.reshape(1), window, slashes, named, q4, kv_chip, halo)
    first = 0
    for n, (pieces, ss) in enumerate(groups):
        state = attend_far(act, q4, state, pieces, first, n == len(groups) - 1)
        first += len(ss)
    context = state[0]

    rows = queries.shape[0]
    ctx_mine = jnp.where(first_core, context[:rows], context[rows:])
    ctx_sib = shift(jnp.where(first_core, context[rows:], context[:rows]), 0, 0, 1)
    ctx = jnp.where(
        first_core,
        jnp.concatenate([ctx_mine, ctx_sib], axis=1),
        jnp.concatenate([ctx_sib, ctx_mine], axis=1),
    )
    partial_value = jnp.dot(ctx, out_weight, preferred_element_type=jnp.float32)

    me = lax.axis_index("tp")
    width = out_weight.shape[1] // 4
    half = width // 2

    def share(step):
        return lax.dynamic_slice_in_dim(partial_value, ((me + step + 4) % 4) * width, width, 1)

    opposite, after, before = share(2), share(1), share(-1)
    via_after = tp_shift(opposite[:, :half].astype(jnp.bfloat16), 1)
    via_before = tp_shift(opposite[:, half:].astype(jnp.bfloat16), -1)
    to_after = jnp.concatenate(
        [after[:, :half] + via_after.astype(jnp.float32), after[:, half:]], axis=1
    ).astype(jnp.bfloat16)
    to_before = jnp.concatenate(
        [before[:, :half], before[:, half:] + via_before.astype(jnp.float32)], axis=1
    ).astype(jnp.bfloat16)
    from_before = tp_shift(to_after, 1)
    from_after = tp_shift(to_before, -1)
    total = share(0) + from_before.astype(jnp.float32) + from_after.astype(jnp.float32)
    return total.astype(jnp.bfloat16)


def solution(mesh):
    return jax.shard_map(
        local,
        mesh=mesh,
        in_specs=(
            P("seq", "tp"),
            P("seq", "tp"),
            P("seq", "tp"),
            P("tp", None),
            P("tp"),
            P("tp", None),
            P("tp", None),
        ),
        out_specs=P("seq", "tp"),
        check_vma=False,
    )
```

```python
import functools
import math

import jax
import jax.numpy as jnp
import numpy as np
from jax import lax
from jax.experimental import pallas as pl
from jax.experimental.pallas import tpu as pltpu
from jax.sharding import PartitionSpec as P

HD = 128
BLK = 128
GROUP = 4
PICKS = 16
NX, NZ = 4, 8
NEG = -1e30
C2 = math.log2(math.e) / math.sqrt(HD)
LIMIT = 100.0
VMEM_BYTES = 40 * 1024 * 1024
SLOT_BITS = 6
BF16, F32, I32 = jnp.bfloat16, jnp.float32, jnp.int32

AX = (0, 3, 1, 2)


def slot_table():
    table = np.zeros((2, NZ, NX), np.int32)

    def put(group, base, same, z, x, at):
        table[same, z % NZ, x % NX] = (group << SLOT_BITS) | (base + at)

    for i, dx in enumerate(AX):
        put(0, 0, 1, 0, dx, i)
        put(0, 4, 1, -1, dx, i)
        put(0, 8, 1, 1, dx, i)
        put(1, 0, 1, -2, dx, i)
        put(1, 4, 1, 2, dx, i)
        put(2, 0, 1, -3, dx, i)
        put(2, 4, 1, 3, dx, i)
        put(2, 8, 1, 4, dx, i)
    for z in range(NZ):
        put(0, 12, 0, z, 0, z)
        put(1, 8, 0, z, -1, z)
        put(1, 16, 0, z, 1, z)
        put(2, 12, 0, z, 2, z)
    return table.reshape(-1)


def seq_at(z, x, core):
    return (z * NX + x) * 2 + core


def along_x(value, dx):
    pairs = [
        (seq_at(z, x, c), seq_at(z, (x + dx) % NX, c))
        for z in range(NZ)
        for x in range(NX)
        for c in range(2)
    ]
    return lax.ppermute(value, "seq", pairs)


def up(value, hop):
    pairs = [
        (seq_at(z, x, c), seq_at(z + 1, x, c))
        for z in range(hop - 1, NZ - 1)
        for x in range(NX)
        for c in range(2)
    ]
    return lax.ppermute(value, "seq", pairs)


def down(value, hop):
    pairs = []
    for source in range(4):
        z = (source - (hop - 1)) % NZ
        pairs += [(z, (z - 1) % NZ)]
    pairs = [
        (seq_at(a, x, c), seq_at(b, x, c)) for a, b in pairs for x in range(NX) for c in range(2)
    ]
    return lax.ppermute(value, "seq", pairs)


def swap_cores(value):
    return lax.ppermute(value, "seq", [(i, i ^ 1) for i in range(2 * NX * NZ)])


def tp_shift(value, step):
    return lax.ppermute(value, "tp", [(i, (i + step) % 4) for i in range(4)])


def dot_f32(a, b, dims):
    return lax.dot_general(a, b, (dims, ((), ())), preferred_element_type=F32)


def lanes(core, width=HD):
    return pl.ds(pl.multiple_of(core * width, width), width)


def chosen_half(blocks, core, shard):
    def look(n, found):
        h = n // PICKS
        hit = blocks[core * GROUP + h, n - h * PICKS] == 2 * shard + 1
        return found | hit.astype(I32)

    return lax.fori_loop(0, GROUP * PICKS, look, 0)


def pick_kernel(of_sibling, scal, blocks, k_ref, v_ref, *outs):
    core, place = scal[0], scal[1]
    shard = place + 1 - 2 * core if of_sibling else place
    half = chosen_half(blocks, core, shard)
    rows = pl.ds(pl.multiple_of(half * BLK, BLK), BLK)
    outs[0][0, :, :HD] = k_ref[rows, lanes(core)]
    outs[0][0, :, HD:] = v_ref[rows, lanes(core)]


def tail_kernel(scal, k_ref, v_ref, k_sib, v_sib, out_ref):
    core = scal[0]

    @pl.when(core == 1)
    def _():
        out_ref[:, :HD] = k_ref[BLK:, HD:]
        out_ref[:, HD:] = v_ref[BLK:, HD:]

    @pl.when(core == 0)
    def _():
        out_ref[:, :HD] = k_sib[BLK:, :HD]
        out_ref[:, HD:] = v_sib[BLK:, :HD]


def split3(m):
    a = m.astype(BF16)
    rest = m - a.astype(F32)
    b = rest.astype(BF16)
    c = (rest - b.astype(F32)).astype(BF16)
    return a, b, c


def extra_columns(m):
    rows = m.shape[0]
    lane = lax.broadcasted_iota(I32, (rows, HD), 1)
    a, b, c = (jnp.broadcast_to(-part.astype(F32), (rows, HD)) for part in split3(m))
    wide = jnp.where(lane == 0, a, jnp.where(lane == 1, b, jnp.where(lane == 2, c, 0.0)))
    return jnp.where(lane == 3, 1.0, wide).astype(BF16)


def local_kernel(
    scal, blocks, win, slash, table, q, q_sib, k, k_sib, v, v_sib, halo,
    qa_ref, acc_ref, list_ref, count_ref, qs, ks, vs, named,
):
    core, place = scal[0], scal[1]
    chip = place // 2
    z, x = chip // NX, chip % NX

    for g in range(16):
        count_ref[g] = 0
    for n in range(GROUP * 8):
        named[n] = 0

    def note(n, carry):
        h = n // PICKS
        b = blocks[core * GROUP + h, n - h * PICKS]
        shard = b // 2
        same = jnp.where(shard % 2 == core, 1, 0)
        from_z = shard // (2 * NX)
        from_x = (shard // 2) % NX
        at_z = jnp.where(same == 1, (from_z - z + NZ) % NZ, from_z)
        entry = table[(same * NZ + at_z) * NX + (from_x - x + NX) % NX]
        group = entry // (1 << SLOT_BITS)
        key = group * GROUP + h
        count = count_ref[key]
        list_ref[key * PICKS + count] = entry - group * (1 << SLOT_BITS)
        count_ref[key] = count + jnp.where(b <= 4 * chip - 2, 1, 0)
        near = b - (4 * chip - 1)
        inside = (near >= 0) & (near < 5)
        at = h * 8 + jnp.where(inside, near, 7)
        named[at] = 1
        return carry

    lax.fori_loop(0, GROUP * PICKS, note, 0)

    mine, sib = core * 2 * BLK, (1 - core) * 2 * BLK
    ks[:BLK] = halo[:, :HD]
    vs[:BLK] = halo[:, HD:]
    for ref, own, other in ((ks, k, k_sib), (vs, v, v_sib)):
        ref[pl.ds(pl.multiple_of(BLK + mine, BLK), 2 * BLK)] = own[:, lanes(core)]
        ref[pl.ds(pl.multiple_of(BLK + sib, BLK), 2 * BLK)] = other[:, lanes(core)]
    for h in range(GROUP):
        cols = pl.ds(pl.multiple_of(core * GROUP * HD + h * HD, HD), HD)
        qs[h, pl.ds(pl.multiple_of(mine, BLK), 2 * BLK)] = q[:, cols]
        qs[h, pl.ds(pl.multiple_of(sib, BLK), 2 * BLK)] = q_sib[:, cols]

    qi = lax.broadcasted_iota(I32, (BLK, BLK), 0)
    kj = lax.broadcasted_iota(I32, (BLK, BLK), 1)
    diag_gap = qi - kj
    prev_gap = diag_gap + BLK
    for h in range(GROUP):
        head = core * GROUP + h
        diag_ok = diag_gap < win[head]
        prev_ok = prev_gap < win[head]
        for n in range(8):
            diag_ok = diag_ok | (diag_gap == slash[head, n])
            prev_ok = prev_ok | (prev_gap == slash[head, n])
        for i in range(4):
            span = (i + 2) * BLK
            rows = slice(i * BLK, (i + 1) * BLK)
            s = dot_f32(qs[h, rows, :], ks[:span], ((1,), (1,)))
            tiles = []
            for t in range(i + 2):
                is_named = named[h * 8 + t] > 0
                if t == i + 1:
                    ok = (diag_gap >= 0) & (diag_ok | is_named)
                elif t == i:
                    ok = prev_ok | is_named
                    if t == 0:
                        ok = ok & (chip > 0)
                else:
                    ok = jnp.broadcast_to(is_named, (BLK, BLK))
                    if t == 0:
                        ok = ok & (chip > 0)
                tiles.append(jnp.where(ok, s[:, t * BLK : (t + 1) * BLK], NEG))
            s = jnp.concatenate(tiles, axis=1)
            m = jnp.max(s, axis=1, keepdims=True)
            w = jnp.exp2((s - m) * C2)
            total = jnp.sum(w, axis=1, keepdims=True)
            acc_ref[h, rows, :HD] = dot_f32(w.astype(BF16), vs[:span], ((1,), (0,)))
            acc_ref[h, rows, HD:] = jnp.broadcast_to(total, (BLK, HD))
            qa_ref[h, rows, :HD] = qs[h, rows, :]
            qa_ref[h, rows, HD:] = extra_columns(m)


def far_kernel(group, sizes, final, scal, lists, counts, qa_in, acc_in, *rest):
    pieces = rest[: len(sizes)]
    if final:
        mine_ref, other_ref, qa_ref, acc_ref, kv, aug, sem = rest[len(sizes) :]
    else:
        qa_ref, acc_ref, kv, aug, sem = rest[len(sizes) :]
    copies = []
    spare = 0
    for n, (piece, size) in enumerate(zip(pieces, sizes)):
        copies.append(pltpu.make_async_copy(piece, kv.at[pl.ds(spare, size)], sem.at[n]))
        spare += size
    for copy in copies:
        copy.start()
    kv[spare] = jnp.zeros((BLK, 2 * HD), BF16)
    lane = lax.broadcasted_iota(I32, (BLK, HD), 1)
    aug[0] = jnp.where(lane < 3, 1.0, jnp.where(lane == 3, NEG, 0.0)).astype(BF16)
    aug[1] = jnp.where(lane < 3, 1.0, 0.0).astype(BF16)
    qa_ref[...] = qa_in[...]
    acc_ref[...] = acc_in[...]
    for copy in copies:
        copy.wait()

    def pair(h, j):
        base = (group * GROUP + h) * PICKS
        count = counts[group * GROUP + h]
        real = jnp.where(2 * j + 1 < count, 1, 0)
        one = lists[base + 2 * j]
        two = jnp.where(real == 1, lists[base + 2 * j + real], spare)
        keys = jnp.concatenate([kv[one, :, :HD], kv[two, :, :HD]], axis=0)
        more = jnp.concatenate([aug[1], aug[real]], axis=0)
        return one, two, dot_f32(qa_ref[h], jnp.concatenate([keys, more], axis=1), ((1,), (1,)))

    def pairs_of(h):
        return (counts[group * GROUP + h] + 1) // 2

    ones = jnp.ones((2 * BLK, HD), BF16)

    def accumulate():
        def head(h, high):
            def step(j, high):
                one, two, s = pair(h, j)
                s = s * C2
                values = jnp.concatenate([kv[one, :, HD:], kv[two, :, HD:]], axis=0)
                acc_ref[h] += dot_f32(
                    jnp.exp2(s).astype(BF16), jnp.concatenate([values, ones], axis=1), ((1,), (0,))
                )
                return jnp.maximum(high, jnp.max(s.reshape(-1, 8, 2 * BLK), axis=0))

            return lax.fori_loop(0, pairs_of(h), step, high)

        return jnp.max(lax.fori_loop(0, GROUP, head, jnp.zeros((8, 2 * BLK), F32)))

    highest = accumulate()

    @pl.when(highest > LIMIT)
    def _():
        def raise_head(h, carry):
            def step(j, gain):
                return jnp.maximum(gain, jnp.max(pair(h, j)[2], axis=1, keepdims=True))

            rows = qa_ref.shape[1]
            gain = lax.fori_loop(0, pairs_of(h), step, jnp.zeros((rows, 1), F32))
            parts = qa_ref[h, :, HD:].astype(F32)
            old = -(parts[:, 0:1] + parts[:, 1:2] + parts[:, 2:3])
            new = old + gain
            qa_ref[h, :, HD:] = extra_columns(new)
            acc_ref[h] = acc_in[h] * jnp.exp2((old - new) * C2)
            return carry

        lax.fori_loop(0, GROUP, raise_head, 0)
        accumulate()

    if final:
        core = scal[0]
        for out, first in ((mine_ref, core * 2 * BLK), (other_ref, (1 - core) * 2 * BLK)):
            rows = pl.ds(pl.multiple_of(first, BLK), 2 * BLK)
            for h in range(GROUP):
                both = acc_ref[h, rows, :]
                out[:, h * HD : (h + 1) * HD] = (both[:, :HD] / both[:, HD:]).astype(BF16)


def weight_tiles(scal, w_ref, w_buf, sem, sibling, rel_tiles):
    core, me = scal[0], scal[2]
    rows, cols = w_buf.shape[1:]
    first = jnp.where(core == (1 if sibling else 0), 0, rows)
    copies = []
    for n, tile in enumerate(rel_tiles):
        step = (2, 1, 3, 0)[tile // 2]
        col = ((me + step) % 4) * (2 * cols) + (tile % 2) * cols
        copies.append(
            pltpu.make_async_copy(
                w_ref.at[pl.ds(pl.multiple_of(first, rows), rows), pl.ds(pl.multiple_of(col, cols), cols)],
                w_buf.at[n],
                sem.at[n],
            )
        )
    for copy in copies:
        copy.start()
    return copies


def own_part_kernel(scal, ctx, w_ref, opp_ref, rest_ref, w_buf, sem):
    copies = weight_tiles(scal, w_ref, w_buf, sem, False, range(8))
    for n, copy in enumerate(copies):
        copy.wait()
        out = opp_ref.at[n] if n < 2 else rest_ref.at[n - 2]
        out[...] = dot_f32(ctx[...], w_buf[n], ((1,), (0,)))


def sib_part_kernel(tiles, scal, ctx, part, w_ref, *rest):
    outs, (w_buf, sem) = rest[: len(tiles)], rest[len(tiles) :]
    copies = weight_tiles(scal, w_ref, w_buf, sem, True, tiles)
    for n, copy in enumerate(copies):
        copy.wait()
        outs[n][...] = (part[n] + dot_f32(ctx[...], w_buf[n], ((1,), (0,)))).astype(outs[n].dtype)


def spec(space):
    return pl.BlockSpec(memory_space=space)


def call(kernel, name, outs, args, spaces, scratch=(), out_spaces=None, flops=0, moved=0):
    return pl.pallas_call(
        kernel,
        out_shape=outs,
        in_specs=[spec(s) for s in spaces],
        out_specs=[spec(s) for s in (out_spaces or [pltpu.VMEM] * len(outs))],
        scratch_shapes=list(scratch),
        compiler_params=pltpu.CompilerParams(vmem_limit_bytes=VMEM_BYTES),
        cost_estimate=pl.CostEstimate(flops=flops, bytes_accessed=moved, transcendentals=0),
        name=name,
    )(*args)


def shape(dims, dtype):
    return jax.ShapeDtypeStruct(dims, dtype)


def local(queries, key_states, value_states, vert_blocks, window_size, slash_offsets, out_weight):
    smem, vmem, anywhere = pltpu.SMEM, pltpu.VMEM, pl.ANY
    place = lax.axis_index("seq").astype(I32)
    me = lax.axis_index("tp").astype(I32)
    core = place % 2
    scal = jnp.stack([core, place, me])
    block = shape((1, BLK, 2 * HD), BF16)

    k_sib = swap_cores(key_states)
    v_sib = swap_cores(value_states)
    q_sib = swap_cores(queries)

    def pick(of_sibling, k, v):
        return call(
            functools.partial(pick_kernel, of_sibling), "pick", [block],
            (scal, vert_blocks, k, v), [smem, smem, vmem, vmem], moved=1_000_000,
        )[0]

    a0 = pick(False, key_states, value_states)
    a = jnp.concatenate([a0, along_x(a0, 1), along_x(a0, -1), along_x(a0, 2)], axis=0)
    b0 = pick(True, k_sib, v_sib)
    b = lax.all_gather(
        b0,
        "seq",
        axis=0,
        tiled=True,
        axis_index_groups=[
            [seq_at(z, x, c) for z in range(NZ)] for x in range(NX) for c in range(2)
        ],
    )
    up1, down1 = up(a, 1), down(a, 1)
    up2, down2 = up(up1, 2), down(down1, 2)
    up3, down3 = up(up2, 3), down(down2, 3)
    up4, down4 = up(up3[:2], 4), down(down3[2:], 4)
    b_right, b_left = along_x(b, 1), along_x(b, -1)
    b_right2, b_left2 = along_x(b_right[:4], 1), along_x(b_left[4:], -1)

    tail = call(
        tail_kernel, "tail", [shape((BLK, 2 * HD), BF16)],
        (scal, key_states, value_states, k_sib, v_sib), [smem] + [vmem] * 4, moved=1_000_000,
    )[0]
    halo = lax.ppermute(tail, "seq", [(i, i + 2) for i in range(2 * NX * NZ - 2)])

    rows = 2 * queries.shape[0]
    wide = (GROUP, rows, 2 * HD)
    qa, acc, lists, counts = call(
        local_kernel,
        "near_part",
        [shape(wide, BF16), shape(wide, F32), shape((16 * PICKS,), I32), shape((16,), I32)],
        (
            scal, vert_blocks, window_size, slash_offsets, jnp.asarray(slot_table()),
            queries, q_sib, key_states, k_sib, value_states, v_sib, halo,
        ),
        [smem] * 5 + [vmem] * 7,
        [
            pltpu.VMEM((GROUP, rows, HD), BF16),
            pltpu.VMEM((rows + BLK, HD), BF16),
            pltpu.VMEM((rows + BLK, HD), BF16),
            pltpu.SMEM((GROUP * 8,), I32),
        ],
        [vmem, vmem, smem, smem],
        flops=1_000_000_000,
        moved=8_000_000,
    )

    groups = [
        [a, up1, down1, b],
        [up2, down2, b_right, b_left],
        [up3, down3, up4, down4, b_right2, b_left2],
    ]
    for n, pieces in enumerate(groups):
        sizes = [p.shape[0] for p in pieces]
        scratch = [
            pltpu.VMEM((sum(sizes) + 1, BLK, 2 * HD), BF16),
            pltpu.VMEM((2, BLK, HD), BF16),
            pltpu.SemaphoreType.DMA((len(sizes),)),
        ]
        final = n == len(groups) - 1
        outs = [shape(wide, BF16), shape(wide, F32)]
        if final:
            scratch = [pltpu.VMEM(wide, BF16), pltpu.VMEM(wide, F32)] + scratch
            outs = [shape((rows // 2, GROUP * HD), BF16)] * 2
        qa, acc = call(
            functools.partial(far_kernel, n, sizes, final),
            "far_part",
            outs,
            (scal, lists, counts, qa, acc, *pieces),
            [smem] * 3 + [vmem] * 2 + [anywhere] * len(sizes),
            scratch,
            flops=1_500_000_000,
            moved=6_000_000,
        )
    ctx_mine, ctx_other = qa, acc
    ctx_sib = swap_cores(ctx_other)

    half_rows, half = rows // 2, out_weight.shape[1] // 8
    depth = GROUP * HD

    def tiles(count, dtype):
        return shape((count, half_rows, half), dtype)

    def w_scratch(count):
        return [pltpu.VMEM((count, depth, half), BF16), pltpu.SemaphoreType.DMA((count,))]

    opp, rest = call(
        own_part_kernel, "own_part", [tiles(2, F32), tiles(6, F32)],
        (scal, ctx_mine, out_weight), [smem, vmem, anywhere], w_scratch(8),
        flops=1_000_000_000, moved=9_000_000,
    )
    tile_bf, tile_f = shape((half_rows, half), BF16), shape((half_rows, half), F32)
    opp0, opp1 = call(
        functools.partial(sib_part_kernel, (0, 1)), "sib_part", [tile_bf] * 2,
        (scal, ctx_sib, opp, out_weight), [smem, vmem, vmem, anywhere], w_scratch(2),
        flops=300_000_000, moved=3_000_000,
    )
    via_before = tp_shift(opp0, 1)
    via_after = tp_shift(opp1, -1)
    after0, after1, before0, before1, own0, own1 = call(
        functools.partial(sib_part_kernel, (2, 3, 4, 5, 6, 7)), "sib_rest",
        [tile_f, tile_bf, tile_bf, tile_f, tile_f, tile_f],
        (scal, ctx_sib, rest, out_weight), [smem, vmem, vmem, anywhere], w_scratch(6),
        flops=800_000_000, moved=9_000_000,
    )
    direct1 = tp_shift(after1, 1)
    direct0 = tp_shift(before0, -1)
    summed0 = tp_shift((after0 + via_before.astype(F32)).astype(BF16), 1)
    summed1 = tp_shift((before1 + via_after.astype(F32)).astype(BF16), -1)
    return jnp.concatenate(
        [
            own0 + direct0.astype(F32) + summed0.astype(F32),
            own1 + direct1.astype(F32) + summed1.astype(F32),
        ],
        axis=1,
    ).astype(BF16)


def solution(mesh):
    return jax.shard_map(
        local,
        mesh=mesh,
        in_specs=(
            P("seq", "tp"),
            P("seq", "tp"),
            P("seq", "tp"),
            P("tp", None),
            P("tp"),
            P("tp", None),
            P("tp", None),
        ),
        out_specs=P("seq", "tp"),
        check_vma=False,
    )
```

```python
import functools
import math

import jax
import jax.numpy as jnp
import numpy as np
from jax import lax
from jax.experimental import pallas as pl
from jax.experimental.pallas import tpu as pltpu
from jax.sharding import PartitionSpec as P

HD = 128
BLK = 128
GROUP = 4
PICKS = 16
NX, NZ = 4, 8
NEG = -1e30
C2 = math.log2(math.e) / math.sqrt(HD)
LIMIT = 100.0
VMEM_BYTES = 40 * 1024 * 1024
SLOT_BITS = 6
AT_ONCE = 4
BF16, F32, I32 = jnp.bfloat16, jnp.float32, jnp.int32

STACKS = ((-1, -2, 1), (-3, -4, 2, 3))


def slot_table():
    table = np.zeros((NZ, NX), np.int32)

    def put(group, base, zs, dx):
        for i, dz in enumerate(zs):
            table[dz % NZ, dx % NX] = (group << SLOT_BITS) | (base + 2 * i)

    first, second = STACKS
    put(0, 0, (0,), 0)
    put(0, 2, first, 0)
    put(0, 8, (0,), -1)
    put(0, 10, (0,), 1)
    put(0, 12, (0,), 2)
    put(0, 14, second, 0)
    put(0, 22, first, -1)
    put(0, 28, first, 1)
    put(1, 0, second, -1)
    put(1, 8, second, 1)
    put(2, 0, first, 2)
    put(2, 6, second, 2)
    return table.reshape(-1)


def seq_at(z, x, core):
    return (z * NX + x) * 2 + core


def along_x(value, dx, lowest):
    pairs = [
        (seq_at(z, x, c), seq_at(z, (x + dx) % NX, c))
        for z in range(lowest, NZ)
        for x in range(NX)
        for c in range(2)
    ]
    return lax.ppermute(value, "seq", pairs)


def along_z(value, dz, lowest, count):
    pairs = [
        (seq_at(z, x, c), seq_at((z + dz) % NZ, x, c))
        for z in range(lowest, lowest + count)
        for x in range(NX)
        for c in range(2)
    ]
    return lax.ppermute(value, "seq", pairs)


def swap_cores(value):
    return lax.ppermute(value, "seq", [(i, i ^ 1) for i in range(2 * NX * NZ)])


def tp_shift(value, step):
    return lax.ppermute(value, "tp", [(i, (i + step) % 4) for i in range(4)])


def dot_f32(a, b, dims):
    return lax.dot_general(a, b, (dims, ((), ())), preferred_element_type=F32)


def lanes(core, width=HD):
    return pl.ds(pl.multiple_of(core * width, width), width)


def pick_kernel(scal, blocks, k_ref, v_ref, k_sib, v_sib, out_ref):
    core, place = scal[0], scal[1]
    head = lax.broadcasted_iota(I32, blocks.shape, 0)
    of_core = (head >= core * GROUP) & (head < (core + 1) * GROUP)
    for k, v, parity in ((k_ref, v_ref, core), (k_sib, v_sib, 1 - core)):
        shard = place - core + parity
        hit = jnp.where(of_core & (blocks[...] == 2 * shard + 1), 1.0, 0.0)
        half = (jnp.max(hit) > 0.5).astype(I32)
        rows = pl.ds(pl.multiple_of(half * BLK, BLK), BLK)
        out_ref[parity, :, :HD] = k[rows, lanes(core)]
        out_ref[parity, :, HD:] = v[rows, lanes(core)]


def tail_kernel(scal, k_ref, v_ref, k_sib, v_sib, out_ref):
    core = scal[0]

    @pl.when(core == 1)
    def _():
        out_ref[:, :HD] = k_ref[BLK:, HD:]
        out_ref[:, HD:] = v_ref[BLK:, HD:]

    @pl.when(core == 0)
    def _():
        out_ref[:, :HD] = k_sib[BLK:, :HD]
        out_ref[:, HD:] = v_sib[BLK:, :HD]


def split3(m):
    a = m.astype(BF16)
    rest = m - a.astype(F32)
    b = rest.astype(BF16)
    c = (rest - b.astype(F32)).astype(BF16)
    return a, b, c


def extra_columns(m):
    rows = m.shape[0]
    lane = lax.broadcasted_iota(I32, (rows, HD), 1)
    a, b, c = (jnp.broadcast_to(-part.astype(F32), (rows, HD)) for part in split3(m))
    wide = jnp.where(lane == 0, a, jnp.where(lane == 1, b, jnp.where(lane == 2, c, 0.0)))
    return jnp.where(lane == 3, 1.0, wide).astype(BF16)


def local_kernel(
    scal, blocks, win, slash, table, q, q_sib, k, k_sib, v, v_sib, halo,
    qa_ref, acc_ref, list_ref, count_ref, qs, ks, vs, named,
):
    core, place = scal[0], scal[1]
    chip = place >> 1
    z, x = chip >> 2, chip & 3

    for g in range(16):
        count_ref[g] = 0
    for n in range(GROUP * 8):
        named[n] = 0

    def note(n, carry):
        h, column = n >> 4, n & 15
        b = blocks[core * GROUP + h, column]
        entry = table[((((b >> 4) - z) & 7) << 2) + (((b >> 2) - x) & 3)]
        key = ((entry >> SLOT_BITS) << 2) + h
        count = count_ref[key]
        list_ref[(key << 4) + count] = (entry & ((1 << SLOT_BITS) - 1)) + ((b >> 1) & 1)
        near = b - (4 * chip - 1)
        count_ref[key] = count + jnp.where(near < 0, 1, 0)
        inside = (near >= 0) & (near < 5)
        named[(h << 3) + jnp.where(inside, near, 7)] = 1
        return carry

    lax.fori_loop(0, GROUP * PICKS, note, 0, unroll=4)

    mine, sib = core * 2 * BLK, (1 - core) * 2 * BLK
    ks[:BLK] = halo[:, :HD]
    vs[:BLK] = halo[:, HD:]
    for ref, own, other in ((ks, k, k_sib), (vs, v, v_sib)):
        ref[pl.ds(pl.multiple_of(BLK + mine, BLK), 2 * BLK)] = own[:, lanes(core)]
        ref[pl.ds(pl.multiple_of(BLK + sib, BLK), 2 * BLK)] = other[:, lanes(core)]
    for h in range(GROUP):
        cols = pl.ds(pl.multiple_of(core * GROUP * HD + h * HD, HD), HD)
        qs[h, pl.ds(pl.multiple_of(mine, BLK), 2 * BLK)] = q[:, cols]
        qs[h, pl.ds(pl.multiple_of(sib, BLK), 2 * BLK)] = q_sib[:, cols]

    qi = lax.broadcasted_iota(I32, (BLK, BLK), 0)
    kj = lax.broadcasted_iota(I32, (BLK, BLK), 1)
    diag_gap = qi - kj
    prev_gap = diag_gap + BLK
    for h in range(GROUP):
        head = core * GROUP + h
        diag_ok = diag_gap < win[head]
        prev_ok = prev_gap < win[head]
        for n in range(8):
            diag_ok = diag_ok | (diag_gap == slash[head, n])
            prev_ok = prev_ok | (prev_gap == slash[head, n])
        scores = dot_f32(qs[h], ks[...], ((1,), (1,)))
        weights = []
        for i in range(4):
            rows = slice(i * BLK, (i + 1) * BLK)
            tiles = []
            for t in range(i + 2):
                is_named = named[h * 8 + t] > 0
                if t == i + 1:
                    ok = (diag_gap >= 0) & (diag_ok | is_named)
                elif t == i:
                    ok = prev_ok | is_named
                else:
                    ok = jnp.broadcast_to(is_named, (BLK, BLK))
                if t == 0:
                    ok = ok & (chip > 0)
                tiles.append(jnp.where(ok, scores[rows, t * BLK : (t + 1) * BLK], NEG))
            m = jnp.max(functools.reduce(jnp.maximum, tiles), axis=1, keepdims=True)
            tiles = [jnp.exp2((tile - m) * C2) for tile in tiles]
            total = jnp.sum(functools.reduce(jnp.add, tiles), axis=1, keepdims=True)
            acc_ref[h, rows, HD:] = jnp.broadcast_to(total, (BLK, HD))
            qa_ref[h, rows, :HD] = qs[h, rows, :]
            qa_ref[h, rows, HD:] = extra_columns(m)
            tiles += [jnp.zeros((BLK, BLK), F32)] * (3 - i)
            weights.append(jnp.concatenate([tile.astype(BF16) for tile in tiles], axis=1))
        acc_ref[h, :, :HD] = dot_f32(jnp.concatenate(weights, axis=0), vs[...], ((1,), (0,)))


def far_kernel(group, sizes, final, scal, lists, counts, qa_in, acc_in, *rest):
    pieces = rest[: len(sizes)]
    if final:
        mine_ref, other_ref, qa_ref, acc_ref, kv, aug, todo, sem = rest[len(sizes) :]
    else:
        qa_ref, acc_ref, kv, aug, todo, sem = rest[len(sizes) :]
    copies = []
    spare = 0
    for n, (piece, size) in enumerate(zip(pieces, sizes)):
        copies.append(pltpu.make_async_copy(piece, kv.at[pl.ds(spare, size)], sem.at[n]))
        spare += size
    for copy in copies:
        copy.start()
    kv[spare] = jnp.zeros((BLK, 2 * HD), BF16)
    lane = lax.broadcasted_iota(I32, (BLK, HD), 1)
    aug[0] = jnp.where(lane < 3, 1.0, jnp.where(lane == 3, NEG, 0.0)).astype(BF16)
    aug[1] = jnp.where(lane < 3, 1.0, 0.0).astype(BF16)
    qa_ref[...] = qa_in[...]
    acc_ref[...] = acc_in[...]

    total = jnp.int32(0)
    for h in range(GROUP):
        base = (group * GROUP + h) * PICKS
        count = counts[group * GROUP + h]

        def note(j, at, h=h, base=base, count=count):
            todo[3 * at] = h
            todo[3 * at + 1] = lists[base + 2 * j]
            more = 2 * j + 1 < count
            todo[3 * at + 2] = jnp.where(more, lists[base + 2 * j + jnp.where(more, 1, 0)], spare)
            return at + 1

        total = lax.fori_loop(0, (count + 1) >> 1, note, total)
    for n in range(AT_ONCE - 1):
        todo[3 * (total + n)] = n
        todo[3 * (total + n) + 1] = spare
        todo[3 * (total + n) + 2] = spare
    steps = (total + AT_ONCE - 1) // AT_ONCE
    for copy in copies:
        copy.wait()

    def entries(i):
        first = 3 * AT_ONCE * i
        return [tuple(todo[first + 3 * n + k] for k in range(3)) for n in range(AT_ONCE)]

    def scores(h, one, two):
        keys = jnp.concatenate([kv[one, :, :HD], kv[two, :, :HD]], axis=0)
        real = [jnp.where(slot == spare, 0, 1) for slot in (one, two)]
        more = jnp.concatenate([aug[real[0]], aug[real[1]]], axis=0)
        return dot_f32(qa_ref[h], jnp.concatenate([keys, more], axis=1), ((1,), (1,)))

    ones = jnp.ones((2 * BLK, HD), BF16)

    def accumulate():
        def step(i, high):
            work = entries(i)
            for h, one, two in work:
                s = scores(h, one, two) * C2
                values = jnp.concatenate([kv[one, :, HD:], kv[two, :, HD:]], axis=0)
                acc_ref[h] += dot_f32(
                    jnp.exp2(s).astype(BF16), jnp.concatenate([values, ones], axis=1), ((1,), (0,))
                )
                high = jnp.maximum(high, jnp.max(s.reshape(-1, 8, 2 * BLK), axis=0))
            return high

        return jnp.max(lax.fori_loop(0, steps, step, jnp.zeros((8, 2 * BLK), F32)))

    highest = accumulate()

    @pl.when(highest > LIMIT)
    def _():
        rows = qa_ref.shape[1]
        for h in range(GROUP):

            def step(n, gain, h=h):
                mine = todo[3 * n] == h
                s = scores(todo[3 * n], todo[3 * n + 1], todo[3 * n + 2])
                top = jnp.max(s, axis=1, keepdims=True)
                return jnp.maximum(gain, jnp.where(mine, top, 0.0))

            gain = lax.fori_loop(0, total, step, jnp.zeros((rows, 1), F32))
            parts = qa_ref[h, :, HD:].astype(F32)
            old = -(parts[:, 0:1] + parts[:, 1:2] + parts[:, 2:3])
            new = old + gain
            qa_ref[h, :, HD:] = extra_columns(new)
            acc_ref[h] = acc_in[h] * jnp.exp2((old - new) * C2)
        accumulate()

    if final:
        core = scal[0]
        for out, first in ((other_ref, (1 - core) * 2 * BLK), (mine_ref, core * 2 * BLK)):
            rows = pl.ds(pl.multiple_of(first, BLK), 2 * BLK)
            for h in range(GROUP):
                both = acc_ref[h, rows, :]
                out[:, h * HD : (h + 1) * HD] = (both[:, :HD] / both[:, HD:]).astype(BF16)


def weight_tiles(scal, w_ref, w_buf, sem, sibling, rel_tiles):
    core, me = scal[0], scal[2]
    rows, cols = w_buf.shape[1:]
    first = jnp.where(core == (1 if sibling else 0), 0, rows)
    copies = []
    for n, tile in enumerate(rel_tiles):
        step = (2, 1, 3, 0)[tile // 2]
        col = ((me + step) % 4) * (2 * cols) + (tile % 2) * cols
        copies.append(
            pltpu.make_async_copy(
                w_ref.at[pl.ds(pl.multiple_of(first, rows), rows), pl.ds(pl.multiple_of(col, cols), cols)],
                w_buf.at[n],
                sem.at[n],
            )
        )
    for copy in copies:
        copy.start()
    return copies


def part_kernel(sibling, tiles, scal, ctx, w_ref, out_ref, w_buf, sem):
    copies = weight_tiles(scal, w_ref, w_buf, sem, sibling, tiles)
    for n, copy in enumerate(copies):
        copy.wait()
        out_ref[n] = dot_f32(ctx[...], w_buf[n], ((1,), (0,)))


def add_part_kernel(sibling, tiles, scal, ctx, part, w_ref, *rest):
    outs, (w_buf, sem) = rest[: len(tiles)], rest[len(tiles) :]
    copies = weight_tiles(scal, w_ref, w_buf, sem, sibling, tiles)
    for n, copy in enumerate(copies):
        copy.wait()
        outs[n][...] = (part[n] + dot_f32(ctx[...], w_buf[n], ((1,), (0,)))).astype(outs[n].dtype)


def both_parts_kernel(tiles, scal, ctx, ctx_sib, w_ref, *rest):
    outs, (w_own, w_sib, sem_own, sem_sib) = rest[: len(tiles)], rest[len(tiles) :]
    own = weight_tiles(scal, w_ref, w_own, sem_own, False, tiles)
    sib = weight_tiles(scal, w_ref, w_sib, sem_sib, True, tiles)
    for n in range(len(tiles)):
        own[n].wait()
        part = dot_f32(ctx[...], w_own[n], ((1,), (0,)))
        sib[n].wait()
        outs[n][...] = (part + dot_f32(ctx_sib[...], w_sib[n], ((1,), (0,)))).astype(outs[n].dtype)


def spec(space):
    return pl.BlockSpec(memory_space=space)


def call(kernel, name, outs, args, spaces, scratch=(), out_spaces=None, flops=0, moved=0):
    return pl.pallas_call(
        kernel,
        out_shape=outs,
        in_specs=[spec(s) for s in spaces],
        out_specs=[spec(s) for s in (out_spaces or [pltpu.VMEM] * len(outs))],
        scratch_shapes=list(scratch),
        compiler_params=pltpu.CompilerParams(vmem_limit_bytes=VMEM_BYTES),
        cost_estimate=pl.CostEstimate(flops=flops, bytes_accessed=moved, transcendentals=0),
        name=name,
    )(*args)


def shape(dims, dtype):
    return jax.ShapeDtypeStruct(dims, dtype)


def local(queries, key_states, value_states, vert_blocks, window_size, slash_offsets, out_weight):
    smem, vmem, anywhere = pltpu.SMEM, pltpu.VMEM, pl.ANY
    place = lax.axis_index("seq").astype(I32)
    me = lax.axis_index("tp").astype(I32)
    core = place % 2
    scal = jnp.stack([core, place, me])
    block = shape((1, BLK, 2 * HD), BF16)

    k_sib = swap_cores(key_states)
    v_sib = swap_cores(value_states)
    q_sib = swap_cores(queries)
    unit = call(
        pick_kernel, "pick", [shape((2, BLK, 2 * HD), BF16)],
        (scal, vert_blocks, key_states, value_states, k_sib, v_sib), [smem] + [vmem] * 5,
        moved=1_000_000,
    )[0]

    up1 = along_z(unit, 1, 0, NZ - 1)
    down1 = along_z(unit, -1, 0, 1)
    up2 = along_z(unit, 2, 0, NZ - 2)
    down2 = along_z(unit, -2, 0, 2)
    down3 = along_z(unit, -3, 0, 3)
    right0, left0 = along_x(unit, 1, 0), along_x(unit, -1, 0)
    up3 = along_z(up2, 1, 2, NZ - 3)
    up4 = along_z(up2, 2, 2, NZ - 4)
    opposite0 = along_x(right0, 1, 0)
    first = jnp.concatenate([up1, up2, down1], axis=0)
    right1, left1 = along_x(first, 1, 1), along_x(first, -1, 1)
    second = jnp.concatenate([up3, up4, down2, down3], axis=0)

    tail = call(
        tail_kernel, "tail", [shape((BLK, 2 * HD), BF16)],
        (scal, key_states, value_states, k_sib, v_sib), [smem] + [vmem] * 4, moved=1_000_000,
    )[0]
    halo = lax.ppermute(tail, "seq", [(i, i + 2) for i in range(2 * NX * NZ - 2)])

    rows = 2 * queries.shape[0]
    wide = (GROUP, rows, 2 * HD)
    qa, acc, lists, counts = call(
        local_kernel,
        "near_part",
        [shape(wide, BF16), shape(wide, F32), shape((16 * PICKS,), I32), shape((16,), I32)],
        (
            scal, vert_blocks, window_size, slash_offsets, jnp.asarray(slot_table()),
            queries, q_sib, key_states, k_sib, value_states, v_sib, halo,
        ),
        [smem] * 5 + [vmem] * 7,
        [
            pltpu.VMEM((GROUP, rows, HD), BF16),
            pltpu.VMEM((rows + BLK, HD), BF16),
            pltpu.VMEM((rows + BLK, HD), BF16),
            pltpu.SMEM((GROUP * 8,), I32),
        ],
        [vmem, vmem, smem, smem],
        flops=1_000_000_000,
        moved=8_000_000,
    )

    def far(n, pieces, qa, acc):
        sizes = [p.shape[0] for p in pieces]
        scratch = [
            pltpu.VMEM((sum(sizes) + 1, BLK, 2 * HD), BF16),
            pltpu.VMEM((2, BLK, HD), BF16),
            pltpu.SMEM((3 * (GROUP * PICKS + AT_ONCE),), I32),
            pltpu.SemaphoreType.DMA((len(sizes),)),
        ]
        final = n == 2
        outs = [shape(wide, BF16), shape(wide, F32)]
        if final:
            scratch = [pltpu.VMEM(wide, BF16), pltpu.VMEM(wide, F32)] + scratch
            outs = [shape((rows // 2, GROUP * HD), BF16)] * 2
        return call(
            functools.partial(far_kernel, n, sizes, final),
            "far_part",
            outs,
            (scal, lists, counts, qa, acc, *pieces),
            [smem] * 3 + [vmem] * 2 + [anywhere] * len(sizes),
            scratch,
            flops=1_500_000_000,
            moved=6_000_000,
        )

    second, acc = lax.optimization_barrier((second, acc))
    right2, left2 = along_x(second, 1, 3), along_x(second, -1, 3)
    opposite1 = along_x(right1, 1, 1)
    qa, acc = far(0, [unit, first, right0, left0, opposite0, second, right1, left1], qa, acc)
    relayed, acc = lax.optimization_barrier((left2, acc))
    opposite2 = along_x(relayed, -1, 3)
    qa, acc = far(1, [right2, left2], qa, acc)
    ctx_mine, ctx_other = far(2, [opposite1, opposite2], qa, acc)
    ctx_sib = swap_cores(ctx_other)

    half_rows, half = rows // 2, out_weight.shape[1] // 8
    depth = GROUP * HD

    def w_scratch(count):
        return [pltpu.VMEM((count, depth, half), BF16)], [pltpu.SemaphoreType.DMA((count,))]

    tile_bf, tile_f = shape((half_rows, half), BF16), shape((half_rows, half), F32)
    opp = call(
        functools.partial(part_kernel, False, (0, 1)), "own_part",
        [shape((2, half_rows, half), F32)], (scal, ctx_mine, out_weight), [smem, vmem, anywhere],
        sum(w_scratch(2), []), flops=300_000_000, moved=3_000_000,
    )[0]
    opp0, opp1 = call(
        functools.partial(add_part_kernel, True, (0, 1)), "sib_part", [tile_bf] * 2,
        (scal, ctx_sib, opp, out_weight), [smem, vmem, vmem, anywhere],
        sum(w_scratch(2), []), flops=300_000_000, moved=3_000_000,
    )
    via_before = tp_shift(opp0, 1)
    via_after = tp_shift(opp1, -1)
    bufs, sems = w_scratch(6)
    after0, after1, before0, before1, own0, own1 = call(
        functools.partial(both_parts_kernel, (2, 3, 4, 5, 6, 7)), "other_shares",
        [tile_f, tile_bf, tile_bf, tile_f, tile_f, tile_f],
        (scal, ctx_mine, ctx_sib, out_weight), [smem, vmem, vmem, anywhere],
        bufs * 2 + sems * 2, flops=1_600_000_000, moved=9_000_000,
    )
    direct1 = tp_shift(after1, 1)
    direct0 = tp_shift(before0, -1)
    summed0 = tp_shift((after0 + via_before.astype(F32)).astype(BF16), 1)
    summed1 = tp_shift((before1 + via_after.astype(F32)).astype(BF16), -1)
    return jnp.concatenate(
        [
            own0 + direct0.astype(F32) + summed0.astype(F32),
            own1 + direct1.astype(F32) + summed1.astype(F32),
        ],
        axis=1,
    ).astype(BF16)


def solution(mesh):
    return jax.shard_map(
        local,
        mesh=mesh,
        in_specs=(
            P("seq", "tp"),
            P("seq", "tp"),
            P("seq", "tp"),
            P("tp", None),
            P("tp"),
            P("tp", None),
            P("tp", None),
        ),
        out_specs=P("seq", "tp"),
        check_vma=False,
    )
```

```python
import functools
import math

import jax
import jax.numpy as jnp
import numpy as np
from jax import lax
from jax.experimental import pallas as pl
from jax.experimental.pallas import tpu as pltpu
from jax.sharding import PartitionSpec as P

HD = 128
BLK = 128
GROUP = 4
PICKS = 16
NX, NZ = 4, 8
NEG = -1e30
C2 = math.log2(math.e) / math.sqrt(HD)
LIMIT = 100.0
VMEM_BYTES = 40 * 1024 * 1024
SLOT_BITS = 6
AT_BLOCKS, AT_WINDOW, AT_SLASH, AT_TABLE = 8, 136, 144, 208
AT_ONCE = 4
BF16, F32, I32 = jnp.bfloat16, jnp.float32, jnp.int32

STACKS = ((0, -1, -2, 1), (-3, -4, 2, 3))


def slot_table():
    table = np.zeros((NZ, NX), np.int32)

    def put(group, base, zs, dx):
        for i, dz in enumerate(zs):
            table[dz % NZ, dx % NX] = (group << SLOT_BITS) | (base + 2 * i)

    first, second = STACKS
    put(0, 0, first, 0)
    put(0, 8, first, -1)
    put(0, 16, first, 1)
    put(0, 24, (0,), 2)
    for at, dz in ((4, -3), (8, -4), (14, 2), (18, 3)):
        put(1, at, (dz,), 0)
    for at, dz in ((2, -1), (6, -2), (10, -3), (12, -4), (16, 1), (20, 2), (22, 3)):
        put(1, at, (dz,), 2)
    put(2, 0, second, -1)
    put(2, 8, second, 1)
    return table.reshape(-1)


def seq_at(z, x, core):
    return (z * NX + x) * 2 + core


def along_x(value, dx, lowest):
    pairs = [
        (seq_at(z, x, c), seq_at(z, (x + dx) % NX, c))
        for z in range(lowest, NZ)
        for x in range(NX)
        for c in range(2)
    ]
    return lax.ppermute(value, "seq", pairs)


def up(value, lowest):
    pairs = [
        (seq_at(z, x, c), seq_at(z + 1, x, c))
        for z in range(lowest, NZ - 1)
        for x in range(NX)
        for c in range(2)
    ]
    return lax.ppermute(value, "seq", pairs)


def down(value, hops):
    steps = sorted({((s - n + 1) % NZ, (s - n) % NZ) for s in range(3) for n in hops})
    pairs = [(seq_at(a, x, c), seq_at(b, x, c)) for a, b in steps for x in range(NX) for c in range(2)]
    return lax.ppermute(value, "seq", pairs)


def swap_cores(value):
    return lax.ppermute(value, "seq", [(i, i ^ 1) for i in range(2 * NX * NZ)])


def tp_shift(value, step):
    return lax.ppermute(value, "tp", [(i, (i + step) % 4) for i in range(4)])


def dot_f32(a, b, dims):
    return lax.dot_general(a, b, (dims, ((), ())), preferred_element_type=F32)


def lanes(core, width=HD):
    return pl.ds(pl.multiple_of(core * width, width), width)


def pick_kernel(scal, blocks, k_ref, v_ref, k_sib, v_sib, out_ref, tail_ref, buf, sem):
    core, place = scal[0], scal[1]
    copies = []
    for n, ref in enumerate((k_ref, v_ref, k_sib, v_sib)):
        copies.append(pltpu.make_async_copy(ref, buf.at[n], sem.at[n]))
    for copy in copies:
        copy.start()
    own, sib = 2 * place + 1, 2 * (place + 1 - 2 * core) + 1

    def look(n, found):
        h = n >> 4
        b = blocks[core * GROUP + h, n & 15]
        return found[0] | (b == own).astype(I32), found[1] | (b == sib).astype(I32)

    zero = jnp.int32(0)
    halves = lax.fori_loop(0, GROUP * PICKS, look, (zero, zero), unroll=8)
    for copy in copies:
        copy.wait()
    for n, parity in enumerate((core, 1 - core)):
        rows = pl.ds(pl.multiple_of(halves[n] * BLK, BLK), BLK)
        out_ref[parity, :, :HD] = buf[2 * n, rows, lanes(core)]
        out_ref[parity, :, HD:] = buf[2 * n + 1, rows, lanes(core)]
    later = 2 * (1 - core)
    tail_ref[:, :HD] = buf[later, BLK:, lanes(core)]
    tail_ref[:, HD:] = buf[later + 1, BLK:, lanes(core)]


def split3(m):
    a = m.astype(BF16)
    rest = m - a.astype(F32)
    b = rest.astype(BF16)
    c = (rest - b.astype(F32)).astype(BF16)
    return a, b, c


def extra_columns(m):
    rows = m.shape[0]
    lane = lax.broadcasted_iota(I32, (rows, HD), 1)
    a, b, c = (jnp.broadcast_to(-part.astype(F32), (rows, HD)) for part in split3(m))
    wide = jnp.where(lane == 0, a, jnp.where(lane == 1, b, jnp.where(lane == 2, c, 0.0)))
    return jnp.where(lane == 3, 1.0, wide).astype(BF16)


def local_kernel(
    ints, q_ref, q_sib_ref, k_ref, k_sib_ref, v_ref, v_sib_ref, halo_ref,
    qa_ref, acc_ref, list_ref, count_ref, q_buf, kv_buf, halo, qs, ks, vs, named, sem,
):
    q, q_sib = q_buf.at[0], q_buf.at[1]
    k, k_sib, v, v_sib = (kv_buf.at[n] for n in range(4))
    copies = [
        pltpu.make_async_copy(source, into, sem.at[n])
        for n, (source, into) in enumerate(
            (
                (q_ref, q), (q_sib_ref, q_sib), (k_ref, k), (k_sib_ref, k_sib),
                (v_ref, v), (v_sib_ref, v_sib), (halo_ref, halo),
            )
        )
    ]
    for copy in copies:
        copy.start()
    core, place = ints[0], ints[1]
    chip = place >> 1
    z, x = chip >> 2, chip & 3

    for g in range(16):
        count_ref[g] = 0
    for n in range(GROUP * 8):
        named[n] = 0

    def note(n, carry):
        h = n >> 4
        b = ints[AT_BLOCKS + core * (GROUP * PICKS) + n]
        entry = ints[AT_TABLE + ((((b >> 4) - z) & 7) << 2) + (((b >> 2) - x) & 3)]
        key = ((entry >> SLOT_BITS) << 2) + h
        count = count_ref[key]
        list_ref[(key << 4) + count] = (entry & ((1 << SLOT_BITS) - 1)) + ((b >> 1) & 1)
        near = b - (4 * chip - 1)
        count_ref[key] = count + jnp.where(near < 0, 1, 0)
        inside = (near >= 0) & (near < 5)
        named[(h << 3) + jnp.where(inside, near, 7)] = 1
        return carry

    lax.fori_loop(0, GROUP * PICKS, note, 0, unroll=4)

    for copy in copies:
        copy.wait()
    mine, sib = core * 2 * BLK, (1 - core) * 2 * BLK
    ks[:BLK] = halo[:, :HD]
    vs[:BLK] = halo[:, HD:]
    for ref, own, other in ((ks, k, k_sib), (vs, v, v_sib)):
        ref[pl.ds(pl.multiple_of(BLK + mine, BLK), 2 * BLK)] = own[:, lanes(core)]
        ref[pl.ds(pl.multiple_of(BLK + sib, BLK), 2 * BLK)] = other[:, lanes(core)]
    for h in range(GROUP):
        cols = pl.ds(pl.multiple_of(core * GROUP * HD + h * HD, HD), HD)
        qs[h, pl.ds(pl.multiple_of(mine, BLK), 2 * BLK)] = q[:, cols]
        qs[h, pl.ds(pl.multiple_of(sib, BLK), 2 * BLK)] = q_sib[:, cols]

    qi = lax.broadcasted_iota(I32, (BLK, BLK), 0)
    kj = lax.broadcasted_iota(I32, (BLK, BLK), 1)
    diag_gap = qi - kj
    prev_gap = diag_gap + BLK
    for h in range(GROUP):
        head = core * GROUP + h
        diag_ok = diag_gap < ints[AT_WINDOW + head]
        prev_ok = prev_gap < ints[AT_WINDOW + head]
        for n in range(8):
            diag_ok = diag_ok | (diag_gap == ints[AT_SLASH + head * 8 + n])
            prev_ok = prev_ok | (prev_gap == ints[AT_SLASH + head * 8 + n])
        scores = dot_f32(qs[h], ks[...], ((1,), (1,)))
        weights = []
        for i in range(4):
            rows = slice(i * BLK, (i + 1) * BLK)
            tiles = []
            for t in range(i + 2):
                is_named = named[h * 8 + t] > 0
                if t == i + 1:
                    ok = (diag_gap >= 0) & (diag_ok | is_named)
                elif t == i:
                    ok = prev_ok | is_named
                else:
                    ok = jnp.broadcast_to(is_named, (BLK, BLK))
                if t == 0:
                    ok = ok & (chip > 0)
                tiles.append(jnp.where(ok, scores[rows, t * BLK : (t + 1) * BLK], NEG))
            m = jnp.max(functools.reduce(jnp.maximum, tiles), axis=1, keepdims=True)
            tiles = [jnp.exp2((tile - m) * C2) for tile in tiles]
            total = jnp.sum(functools.reduce(jnp.add, tiles), axis=1, keepdims=True)
            acc_ref[h, rows, HD:] = jnp.broadcast_to(total, (BLK, HD))
            qa_ref[h, rows, :HD] = qs[h, rows, :]
            qa_ref[h, rows, HD:] = extra_columns(m)
            tiles += [jnp.zeros((BLK, BLK), F32)] * (3 - i)
            weights.append(jnp.concatenate([tile.astype(BF16) for tile in tiles], axis=1))
        acc_ref[h, :, :HD] = dot_f32(jnp.concatenate(weights, axis=0), vs[...], ((1,), (0,)))


def far_kernel(group, sizes, final, scal, lists, counts, qa_in, acc_in, *rest):
    pieces = rest[: len(sizes)]
    if final:
        mine_ref, other_ref, qa_ref, acc_ref, kv, aug, todo, sem = rest[len(sizes) :]
    else:
        qa_ref, acc_ref, kv, aug, todo, sem = rest[len(sizes) :]
    copies = []
    spare = 0
    for n, (piece, size) in enumerate(zip(pieces, sizes)):
        copies.append(pltpu.make_async_copy(piece, kv.at[pl.ds(spare, size)], sem.at[n]))
        spare += size
    for copy in copies:
        copy.start()
    kv[spare] = jnp.zeros((BLK, 2 * HD), BF16)
    lane = lax.broadcasted_iota(I32, (BLK, HD), 1)
    aug[0] = jnp.where(lane < 3, 1.0, jnp.where(lane == 3, NEG, 0.0)).astype(BF16)
    aug[1] = jnp.where(lane < 3, 1.0, 0.0).astype(BF16)
    qa_ref[...] = qa_in[...]
    acc_ref[...] = acc_in[...]

    total = jnp.int32(0)
    for h in range(GROUP):
        base = (group * GROUP + h) * PICKS
        count = counts[group * GROUP + h]

        def note(j, at, h=h, base=base, count=count):
            todo[3 * at] = h
            todo[3 * at + 1] = lists[base + 2 * j]
            more = 2 * j + 1 < count
            todo[3 * at + 2] = jnp.where(more, lists[base + 2 * j + jnp.where(more, 1, 0)], spare)
            return at + 1

        total = lax.fori_loop(0, (count + 1) >> 1, note, total)
    for n in range(AT_ONCE - 1):
        todo[3 * (total + n)] = n
        todo[3 * (total + n) + 1] = spare
        todo[3 * (total + n) + 2] = spare
    steps = (total + AT_ONCE - 1) // AT_ONCE
    for copy in copies:
        copy.wait()

    def entries(i):
        first = 3 * AT_ONCE * i
        return [tuple(todo[first + 3 * n + k] for k in range(3)) for n in range(AT_ONCE)]

    def scores(h, one, two):
        keys = jnp.concatenate([kv[one, :, :HD], kv[two, :, :HD]], axis=0)
        real = [jnp.where(slot == spare, 0, 1) for slot in (one, two)]
        more = jnp.concatenate([aug[real[0]], aug[real[1]]], axis=0)
        return dot_f32(qa_ref[h], jnp.concatenate([keys, more], axis=1), ((1,), (1,)))

    ones = jnp.ones((2 * BLK, HD), BF16)

    def accumulate():
        def step(i, high):
            work = entries(i)
            for h, one, two in work:
                s = scores(h, one, two) * C2
                values = jnp.concatenate([kv[one, :, HD:], kv[two, :, HD:]], axis=0)
                acc_ref[h] += dot_f32(
                    jnp.exp2(s).astype(BF16), jnp.concatenate([values, ones], axis=1), ((1,), (0,))
                )
                high = jnp.maximum(high, jnp.max(s.reshape(-1, 8, 2 * BLK), axis=0))
            return high

        return jnp.max(lax.fori_loop(0, steps, step, jnp.zeros((8, 2 * BLK), F32)))

    highest = accumulate()

    @pl.when(highest > LIMIT)
    def _():
        rows = qa_ref.shape[1]
        for h in range(GROUP):

            def step(n, gain, h=h):
                mine = todo[3 * n] == h
                s = scores(todo[3 * n], todo[3 * n + 1], todo[3 * n + 2])
                top = jnp.max(s, axis=1, keepdims=True)
                return jnp.maximum(gain, jnp.where(mine, top, 0.0))

            gain = lax.fori_loop(0, total, step, jnp.zeros((rows, 1), F32))
            parts = qa_ref[h, :, HD:].astype(F32)
            old = -(parts[:, 0:1] + parts[:, 1:2] + parts[:, 2:3])
            new = old + gain
            qa_ref[h, :, HD:] = extra_columns(new)
            acc_ref[h] = acc_in[h] * jnp.exp2((old - new) * C2)
        accumulate()

    if final:
        core = scal[0]
        for out, first in ((other_ref, (1 - core) * 2 * BLK), (mine_ref, core * 2 * BLK)):
            rows = pl.ds(pl.multiple_of(first, BLK), 2 * BLK)
            for h in range(GROUP):
                both = acc_ref[h, rows, :]
                out[:, h * HD : (h + 1) * HD] = (both[:, :HD] / both[:, HD:]).astype(BF16)


def weight_tiles(scal, w_ref, w_buf, sem, sibling, rel_tiles):
    core, me = scal[0], scal[2]
    rows, cols = w_buf.shape[1:]
    first = jnp.where(core == (1 if sibling else 0), 0, rows)
    copies = []
    for n, tile in enumerate(rel_tiles):
        step = (2, 1, 3, 0)[tile // 2]
        col = ((me + step) % 4) * (2 * cols) + (tile % 2) * cols
        copies.append(
            pltpu.make_async_copy(
                w_ref.at[pl.ds(pl.multiple_of(first, rows), rows), pl.ds(pl.multiple_of(col, cols), cols)],
                w_buf.at[n],
                sem.at[n],
            )
        )
    for copy in copies:
        copy.start()
    return copies


def part_kernel(sibling, tiles, scal, ctx, w_ref, out_ref, w_buf, sem):
    copies = weight_tiles(scal, w_ref, w_buf, sem, sibling, tiles)
    for n, copy in enumerate(copies):
        copy.wait()
        out_ref[n] = dot_f32(ctx[...], w_buf[n], ((1,), (0,)))


def add_part_kernel(sibling, tiles, scal, ctx, part, w_ref, *rest):
    outs, (w_buf, sem) = rest[: len(tiles)], rest[len(tiles) :]
    copies = weight_tiles(scal, w_ref, w_buf, sem, sibling, tiles)
    for n, copy in enumerate(copies):
        copy.wait()
        outs[n][...] = (part[n] + dot_f32(ctx[...], w_buf[n], ((1,), (0,)))).astype(outs[n].dtype)


def both_parts_kernel(tiles, scal, ctx, ctx_sib, w_ref, *rest):
    outs, (w_own, w_sib, sem_own, sem_sib) = rest[: len(tiles)], rest[len(tiles) :]
    own = weight_tiles(scal, w_ref, w_own, sem_own, False, tiles)
    sib = weight_tiles(scal, w_ref, w_sib, sem_sib, True, tiles)
    for n in range(len(tiles)):
        own[n].wait()
        part = dot_f32(ctx[...], w_own[n], ((1,), (0,)))
        sib[n].wait()
        outs[n][...] = (part + dot_f32(ctx_sib[...], w_sib[n], ((1,), (0,)))).astype(outs[n].dtype)


def spec(space):
    return pl.BlockSpec(memory_space=space)


def call(
    kernel, name, outs, args, spaces, scratch=(), out_spaces=None, flops=0, moved=0, vmem_bytes=VMEM_BYTES
):
    return pl.pallas_call(
        kernel,
        out_shape=outs,
        in_specs=[spec(s) for s in spaces],
        out_specs=[spec(s) for s in (out_spaces or [pltpu.VMEM] * len(outs))],
        scratch_shapes=list(scratch),
        compiler_params=pltpu.CompilerParams(vmem_limit_bytes=vmem_bytes),
        cost_estimate=pl.CostEstimate(flops=flops, bytes_accessed=moved, transcendentals=0),
        name=name,
    )(*args)


def shape(dims, dtype):
    return jax.ShapeDtypeStruct(dims, dtype)


def local(queries, key_states, value_states, vert_blocks, window_size, slash_offsets, out_weight):
    smem, vmem, anywhere = pltpu.SMEM, pltpu.VMEM, pl.ANY
    place = lax.axis_index("seq").astype(I32)
    me = lax.axis_index("tp").astype(I32)
    core = place % 2
    scal = jnp.stack([core, place, me])
    ints = jnp.concatenate(
        [
            jnp.pad(scal, (0, AT_BLOCKS - 3)),
            vert_blocks.reshape(-1),
            window_size,
            slash_offsets.reshape(-1),
            jnp.asarray(slot_table()),
        ]
    )
    block = shape((1, BLK, 2 * HD), BF16)

    k_sib = swap_cores(key_states)
    v_sib = swap_cores(value_states)
    q_sib = swap_cores(queries)
    unit, tail = call(
        pick_kernel, "pick", [shape((2, BLK, 2 * HD), BF16), shape((BLK, 2 * HD), BF16)],
        (scal, vert_blocks, key_states, value_states, k_sib, v_sib),
        [smem] * 2 + [anywhere] * 4,
        [pltpu.VMEM((4,) + key_states.shape, BF16), pltpu.SemaphoreType.DMA((4,))],
        moved=1_000_000,
        vmem_bytes=60 * 1024 * 1024,
    )

    halo = lax.ppermute(tail, "seq", [(i, i + 2) for i in range(2 * NX * NZ - 2)])

    up1, down1 = up(unit, 0), down(unit, (1,))
    opposite = along_x(unit, 2, 0)
    up1, halo = lax.optimization_barrier((up1, halo))
    up2 = up(jnp.concatenate([up1, opposite], axis=0), 0)
    down2 = down(jnp.concatenate([down1, opposite], axis=0), (2, 1))
    up3, down3 = up(up2, 1), down(down2, (3, 2))
    first = jnp.concatenate([unit, up1, up2[:2], down1], axis=0)
    right1, left1 = along_x(first, 1, 0), along_x(first, -1, 0)

    rows = 2 * queries.shape[0]
    wide = (GROUP, rows, 2 * HD)
    qa, acc, lists, counts = call(
        local_kernel,
        "near_part",
        [shape(wide, BF16), shape(wide, F32), shape((16 * PICKS,), I32), shape((16,), I32)],
        (
            ints, queries, q_sib, key_states, k_sib, value_states, v_sib, halo,
        ),
        [smem] + [anywhere] * 7,
        [
            pltpu.VMEM((2,) + queries.shape, BF16),
            pltpu.VMEM((4,) + key_states.shape, BF16),
            pltpu.VMEM((BLK, 2 * HD), BF16),
            pltpu.VMEM((GROUP, rows, HD), BF16),
            pltpu.VMEM((rows + BLK, HD), BF16),
            pltpu.VMEM((rows + BLK, HD), BF16),
            pltpu.SMEM((GROUP * 8,), I32),
            pltpu.SemaphoreType.DMA((7,)),
        ],
        [vmem, vmem, smem, smem],
        flops=5_000_000_000,
        moved=100_000,
    )

    def far(n, pieces, qa, acc):
        sizes = [p.shape[0] for p in pieces]
        scratch = [
            pltpu.VMEM((sum(sizes) + 1, BLK, 2 * HD), BF16),
            pltpu.VMEM((2, BLK, HD), BF16),
            pltpu.SMEM((3 * (GROUP * PICKS + AT_ONCE),), I32),
            pltpu.SemaphoreType.DMA((len(sizes),)),
        ]
        final = n == 2
        outs = [shape(wide, BF16), shape(wide, F32)]
        if final:
            scratch = [pltpu.VMEM(wide, BF16), pltpu.VMEM(wide, F32)] + scratch
            outs = [shape((rows // 2, GROUP * HD), BF16)] * 2
        return call(
            functools.partial(far_kernel, n, sizes, final),
            "far_part",
            outs,
            (scal, lists, counts, qa, acc, *pieces),
            [smem] * 3 + [vmem] * 2 + [anywhere] * len(sizes),
            scratch,
            flops=6_000_000_000,
            moved=100_000,
        )

    up4 = up(up3, 2)
    second = jnp.concatenate([up3[:2], up4[:2], down2[:2], down3[:2]], axis=0)
    up5, down4 = up(up4[2:], 3), down(down3[2:], (3,))
    qa, acc = far(0, [first, right1, left1, opposite], qa, acc)
    second, acc = lax.optimization_barrier((second, acc))
    right2, left2 = along_x(second, 1, 3), along_x(second, -1, 3)
    qa, acc = far(1, [up2, up3, up4, up5, down2, down3, down4], qa, acc)
    ctx_mine, ctx_other = far(2, [right2, left2], qa, acc)
    ctx_sib = swap_cores(ctx_other)

    half_rows, half = rows // 2, out_weight.shape[1] // 8
    depth = GROUP * HD

    def w_scratch(count):
        return [pltpu.VMEM((count, depth, half), BF16)], [pltpu.SemaphoreType.DMA((count,))]

    tile_bf, tile_f = shape((half_rows, half), BF16), shape((half_rows, half), F32)
    opp = call(
        functools.partial(part_kernel, False, (0, 1)), "own_part",
        [shape((2, half_rows, half), F32)], (scal, ctx_mine, out_weight), [smem, vmem, anywhere],
        sum(w_scratch(2), []), flops=300_000_000, moved=3_000_000,
    )[0]
    opp0, opp1 = call(
        functools.partial(add_part_kernel, True, (0, 1)), "sib_part", [tile_bf] * 2,
        (scal, ctx_sib, opp, out_weight), [smem, vmem, vmem, anywhere],
        sum(w_scratch(2), []), flops=300_000_000, moved=3_000_000,
    )
    via_before = tp_shift(opp0, 1)
    via_after = tp_shift(opp1, -1)
    bufs, sems = w_scratch(6)
    after0, after1, before0, before1, own0, own1 = call(
        functools.partial(both_parts_kernel, (2, 3, 4, 5, 6, 7)), "other_shares",
        [tile_f, tile_bf, tile_bf, tile_f, tile_f, tile_f],
        (scal, ctx_mine, ctx_sib, out_weight), [smem, vmem, vmem, anywhere],
        bufs * 2 + sems * 2, flops=1_600_000_000, moved=9_000_000,
    )
    direct1 = tp_shift(after1, 1)
    direct0 = tp_shift(before0, -1)
    summed0 = tp_shift((after0 + via_before.astype(F32)).astype(BF16), 1)
    summed1 = tp_shift((before1 + via_after.astype(F32)).astype(BF16), -1)
    return jnp.concatenate(
        [
            own0 + direct0.astype(F32) + summed0.astype(F32),
            own1 + direct1.astype(F32) + summed1.astype(F32),
        ],
        axis=1,
    ).astype(BF16)


def solution(mesh):
    return jax.shard_map(
        local,
        mesh=mesh,
        in_specs=(
            P("seq", "tp"),
            P("seq", "tp"),
            P("seq", "tp"),
            P("tp", None),
            P("tp"),
            P("tp", None),
            P("tp", None),
        ),
        out_specs=P("seq", "tp"),
        check_vma=False,
    )
```

```python
import functools
import math

import jax
import jax.numpy as jnp
import numpy as np
from jax import lax
from jax.experimental import pallas as pl
from jax.experimental.pallas import tpu as pltpu
from jax.sharding import PartitionSpec as P

HD = 128
BLK = 128
GROUP = 4
PICKS = 16
NX, NZ = 4, 8
NEG = -1e30
C2 = math.log2(math.e) / math.sqrt(HD)
LIMIT = 100.0
VMEM_BYTES = 40 * 1024 * 1024
SLOT_BITS = 6
AT_ONCE = 4
BF16, F32, I32 = jnp.bfloat16, jnp.float32, jnp.int32

STACKS = ((0, -1, -2, 1), (-3, -4, 2, 3))


def slot_table():
    table = np.zeros((NZ, NX), np.int32)

    def put(group, base, zs, dx):
        for i, dz in enumerate(zs):
            table[dz % NZ, dx % NX] = (group << SLOT_BITS) | (base + 2 * i)

    first, second = STACKS
    put(0, 0, first, 0)
    put(0, 8, first, -1)
    put(0, 16, first, 1)
    put(0, 24, (0,), 2)
    for at, dz in ((4, -3), (8, -4), (14, 2), (18, 3)):
        put(2, at, (dz,), 0)
    for at, dz in ((2, -1), (6, -2), (10, -3), (12, -4), (16, 1), (20, 2), (22, 3)):
        put(2, at, (dz,), 2)
    put(1, 0, second, -1)
    put(1, 8, second, 1)
    return table.reshape(-1)


def seq_at(z, x, core):
    return (z * NX + x) * 2 + core


def along_x(value, dx, lowest):
    pairs = [
        (seq_at(z, x, c), seq_at(z, (x + dx) % NX, c))
        for z in range(lowest, NZ)
        for x in range(NX)
        for c in range(2)
    ]
    return lax.ppermute(value, "seq", pairs)


def up(value, lowest):
    pairs = [
        (seq_at(z, x, c), seq_at(z + 1, x, c))
        for z in range(lowest, NZ - 1)
        for x in range(NX)
        for c in range(2)
    ]
    return lax.ppermute(value, "seq", pairs)


def down(value, hops):
    steps = sorted({((s - n + 1) % NZ, (s - n) % NZ) for s in range(3) for n in hops})
    pairs = [(seq_at(a, x, c), seq_at(b, x, c)) for a, b in steps for x in range(NX) for c in range(2)]
    return lax.ppermute(value, "seq", pairs)


def swap_cores(value):
    return lax.ppermute(value, "seq", [(i, i ^ 1) for i in range(2 * NX * NZ)])


def tp_shift(value, step):
    return lax.ppermute(value, "tp", [(i, (i + step) % 4) for i in range(4)])


def dot_f32(a, b, dims):
    return lax.dot_general(a, b, (dims, ((), ())), preferred_element_type=F32)


def lanes(core, width=HD):
    return pl.ds(pl.multiple_of(core * width, width), width)


def pick_kernel(scal, blocks_ref, k_ref, v_ref, k_sib, v_sib, out_ref, tail_ref, buf, blocks, sem):
    core, place = scal[0], scal[1]
    copies = []
    for n, ref in enumerate((k_ref, v_ref, k_sib, v_sib)):
        copies.append(pltpu.make_async_copy(ref, buf.at[n], sem.at[n]))
    naming = pltpu.make_async_copy(blocks_ref, blocks, sem.at[4])
    naming.start()
    for copy in copies:
        copy.start()
    naming.wait()
    own, sib = 2 * place + 1, 2 * (place + 1 - 2 * core) + 1

    def look(n, found):
        h = n >> 4
        b = blocks[core * GROUP + h, n & 15]
        return found[0] | (b == own).astype(I32), found[1] | (b == sib).astype(I32)

    zero = jnp.int32(0)
    halves = lax.fori_loop(0, GROUP * PICKS, look, (zero, zero), unroll=8)
    for copy in copies:
        copy.wait()
    for n, parity in enumerate((core, 1 - core)):
        rows = pl.ds(pl.multiple_of(halves[n] * BLK, BLK), BLK)
        out_ref[parity, :, :HD] = buf[2 * n, rows, lanes(core)]
        out_ref[parity, :, HD:] = buf[2 * n + 1, rows, lanes(core)]
    later = 2 * (1 - core)
    tail_ref[:, :HD] = buf[later, BLK:, lanes(core)]
    tail_ref[:, HD:] = buf[later + 1, BLK:, lanes(core)]


def split3(m):
    a = m.astype(BF16)
    rest = m - a.astype(F32)
    b = rest.astype(BF16)
    c = (rest - b.astype(F32)).astype(BF16)
    return a, b, c


def extra_columns(m):
    rows = m.shape[0]
    lane = lax.broadcasted_iota(I32, (rows, HD), 1)
    a, b, c = (jnp.broadcast_to(-part.astype(F32), (rows, HD)) for part in split3(m))
    wide = jnp.where(lane == 0, a, jnp.where(lane == 1, b, jnp.where(lane == 2, c, 0.0)))
    return jnp.where(lane == 3, 1.0, wide).astype(BF16)


def local_kernel(
    scal, blocks, window, slash, table, q_ref, q_sib_ref, k_ref, k_sib_ref, v_ref, v_sib_ref, halo_ref,
    qa_ref, acc_ref, list_ref, count_ref, q_buf, kv_buf, halo, qs, ks, vs, named, sem,
):
    q, q_sib = q_buf.at[0], q_buf.at[1]
    k, k_sib, v, v_sib = (kv_buf.at[n] for n in range(4))
    copies = [
        pltpu.make_async_copy(source, into, sem.at[n])
        for n, (source, into) in enumerate(
            (
                (q_ref, q), (q_sib_ref, q_sib), (k_ref, k), (k_sib_ref, k_sib),
                (v_ref, v), (v_sib_ref, v_sib), (halo_ref, halo),
            )
        )
    ]
    for copy in copies:
        copy.start()
    core, place = scal[0], scal[1]
    chip = place >> 1
    z, x = chip >> 2, chip & 3

    for g in range(16):
        count_ref[g] = 0
    for n in range(GROUP * 8):
        named[n] = 0

    def note(n, carry):
        h = n >> 4
        b = blocks[core * GROUP + h, n & 15]
        entry = table[((((b >> 4) - z) & 7) << 2) + (((b >> 2) - x) & 3)]
        key = ((entry >> SLOT_BITS) << 2) + h
        count = count_ref[key]
        list_ref[(key << 4) + count] = (entry & ((1 << SLOT_BITS) - 1)) + ((b >> 1) & 1)
        near = b - (4 * chip - 1)
        count_ref[key] = count + jnp.where(near < 0, 1, 0)
        inside = (near >= 0) & (near < 5)
        named[(h << 3) + jnp.where(inside, near, 7)] = 1
        return carry

    lax.fori_loop(0, GROUP * PICKS, note, 0, unroll=4)

    for copy in copies:
        copy.wait()
    mine, sib = core * 2 * BLK, (1 - core) * 2 * BLK
    ks[:BLK] = halo[:, :HD]
    vs[:BLK] = halo[:, HD:]
    for ref, own, other in ((ks, k, k_sib), (vs, v, v_sib)):
        ref[pl.ds(pl.multiple_of(BLK + mine, BLK), 2 * BLK)] = own[:, lanes(core)]
        ref[pl.ds(pl.multiple_of(BLK + sib, BLK), 2 * BLK)] = other[:, lanes(core)]
    for h in range(GROUP):
        cols = pl.ds(pl.multiple_of(core * GROUP * HD + h * HD, HD), HD)
        qs[h, pl.ds(pl.multiple_of(mine, BLK), 2 * BLK)] = q[:, cols]
        qs[h, pl.ds(pl.multiple_of(sib, BLK), 2 * BLK)] = q_sib[:, cols]

    qi = lax.broadcasted_iota(I32, (BLK, BLK), 0)
    kj = lax.broadcasted_iota(I32, (BLK, BLK), 1)
    diag_gap = qi - kj
    prev_gap = diag_gap + BLK
    for h in range(GROUP):
        head = core * GROUP + h
        diag_ok = diag_gap < window[head]
        prev_ok = prev_gap < window[head]
        for n in range(8):
            diag_ok = diag_ok | (diag_gap == slash[head, n])
            prev_ok = prev_ok | (prev_gap == slash[head, n])
        scores = dot_f32(qs[h], ks[...], ((1,), (1,)))
        weights = []
        for i in range(4):
            rows = slice(i * BLK, (i + 1) * BLK)
            tiles = []
            for t in range(i + 2):
                is_named = named[h * 8 + t] > 0
                if t == i + 1:
                    ok = (diag_gap >= 0) & (diag_ok | is_named)
                elif t == i:
                    ok = prev_ok | is_named
                else:
                    ok = jnp.broadcast_to(is_named, (BLK, BLK))
                if t == 0:
                    ok = ok & (chip > 0)
                tiles.append(jnp.where(ok, scores[rows, t * BLK : (t + 1) * BLK], NEG))
            m = jnp.max(functools.reduce(jnp.maximum, tiles), axis=1, keepdims=True)
            tiles = [jnp.exp2((tile - m) * C2) for tile in tiles]
            total = jnp.sum(functools.reduce(jnp.add, tiles), axis=1, keepdims=True)
            acc_ref[h, rows, HD:] = jnp.broadcast_to(total, (BLK, HD))
            qa_ref[h, rows, :HD] = qs[h, rows, :]
            qa_ref[h, rows, HD:] = extra_columns(m)
            tiles += [jnp.zeros((BLK, BLK), F32)] * (3 - i)
            weights.append(jnp.concatenate([tile.astype(BF16) for tile in tiles], axis=1))
        acc_ref[h, :, :HD] = dot_f32(jnp.concatenate(weights, axis=0), vs[...], ((1,), (0,)))


def far_kernel(group, sizes, final, scal, lists, counts, qa_in, acc_in, *rest):
    pieces = rest[: len(sizes)]
    if final:
        mine_ref, other_ref, qa_ref, acc_ref, kv, aug, todo, sem = rest[len(sizes) :]
    else:
        qa_ref, acc_ref, kv, aug, todo, sem = rest[len(sizes) :]
    copies = []
    spare = 0
    for n, (piece, size) in enumerate(zip(pieces, sizes)):
        copies.append(pltpu.make_async_copy(piece, kv.at[pl.ds(spare, size)], sem.at[n]))
        spare += size
    for copy in copies:
        copy.start()
    kv[spare] = jnp.zeros((BLK, 2 * HD), BF16)
    lane = lax.broadcasted_iota(I32, (BLK, HD), 1)
    aug[0] = jnp.where(lane < 3, 1.0, jnp.where(lane == 3, NEG, 0.0)).astype(BF16)
    aug[1] = jnp.where(lane < 3, 1.0, 0.0).astype(BF16)
    qa_ref[...] = qa_in[...]
    acc_ref[...] = acc_in[...]

    total = jnp.int32(0)
    for h in range(GROUP):
        base = (group * GROUP + h) * PICKS
        count = counts[group * GROUP + h]

        def note(j, at, h=h, base=base, count=count):
            todo[3 * at] = h
            todo[3 * at + 1] = lists[base + 2 * j]
            more = 2 * j + 1 < count
            todo[3 * at + 2] = jnp.where(more, lists[base + 2 * j + jnp.where(more, 1, 0)], spare)
            return at + 1

        total = lax.fori_loop(0, (count + 1) >> 1, note, total)
    for n in range(AT_ONCE - 1):
        todo[3 * (total + n)] = n
        todo[3 * (total + n) + 1] = spare
        todo[3 * (total + n) + 2] = spare
    steps = (total + AT_ONCE - 1) // AT_ONCE
    for copy in copies:
        copy.wait()

    def entries(i):
        first = 3 * AT_ONCE * i
        return [tuple(todo[first + 3 * n + k] for k in range(3)) for n in range(AT_ONCE)]

    def scores(h, one, two):
        keys = jnp.concatenate([kv[one, :, :HD], kv[two, :, :HD]], axis=0)
        real = [jnp.where(slot == spare, 0, 1) for slot in (one, two)]
        more = jnp.concatenate([aug[real[0]], aug[real[1]]], axis=0)
        return dot_f32(qa_ref[h], jnp.concatenate([keys, more], axis=1), ((1,), (1,)))

    ones = jnp.ones((2 * BLK, HD), BF16)

    def accumulate():
        def step(i, high):
            work = entries(i)
            for h, one, two in work:
                s = scores(h, one, two) * C2
                values = jnp.concatenate([kv[one, :, HD:], kv[two, :, HD:]], axis=0)
                acc_ref[h] += dot_f32(
                    jnp.exp2(s).astype(BF16), jnp.concatenate([values, ones], axis=1), ((1,), (0,))
                )
                high = jnp.maximum(high, jnp.max(s.reshape(-1, 8, 2 * BLK), axis=0))
            return high

        return jnp.max(lax.fori_loop(0, steps, step, jnp.zeros((8, 2 * BLK), F32)))

    highest = accumulate()

    @pl.when(highest > LIMIT)
    def _():
        rows = qa_ref.shape[1]
        for h in range(GROUP):

            def step(n, gain, h=h):
                mine = todo[3 * n] == h
                s = scores(todo[3 * n], todo[3 * n + 1], todo[3 * n + 2])
                top = jnp.max(s, axis=1, keepdims=True)
                return jnp.maximum(gain, jnp.where(mine, top, 0.0))

            gain = lax.fori_loop(0, total, step, jnp.zeros((rows, 1), F32))
            parts = qa_ref[h, :, HD:].astype(F32)
            old = -(parts[:, 0:1] + parts[:, 1:2] + parts[:, 2:3])
            new = old + gain
            qa_ref[h, :, HD:] = extra_columns(new)
            acc_ref[h] = acc_in[h] * jnp.exp2((old - new) * C2)
        accumulate()

    if final:
        core = scal[0]
        for out, first in ((other_ref, (1 - core) * 2 * BLK), (mine_ref, core * 2 * BLK)):
            rows = pl.ds(pl.multiple_of(first, BLK), 2 * BLK)
            for h in range(GROUP):
                both = acc_ref[h, rows, :]
                out[:, h * HD : (h + 1) * HD] = (both[:, :HD] / both[:, HD:]).astype(BF16)


def crossed_kernel(right, left, out_ref):
    out_ref[...] = jnp.zeros_like(out_ref)


def weight_tiles(scal, w_ref, w_buf, sem, sibling, rel_tiles):
    core, me = scal[0], scal[2]
    rows, cols = w_buf.shape[1:]
    first = jnp.where(core == (1 if sibling else 0), 0, rows)
    copies = []
    for n, tile in enumerate(rel_tiles):
        step = (2, 1, 3, 0)[tile // 2]
        col = ((me + step) % 4) * (2 * cols) + (tile % 2) * cols
        copies.append(
            pltpu.make_async_copy(
                w_ref.at[pl.ds(pl.multiple_of(first, rows), rows), pl.ds(pl.multiple_of(col, cols), cols)],
                w_buf.at[n],
                sem.at[n],
            )
        )
    for copy in copies:
        copy.start()
    return copies


def part_kernel(sibling, tiles, scal, ctx, w_ref, out_ref, w_buf, sem):
    copies = weight_tiles(scal, w_ref, w_buf, sem, sibling, tiles)
    for n, copy in enumerate(copies):
        copy.wait()
        out_ref[n] = dot_f32(ctx[...], w_buf[n], ((1,), (0,)))


def add_part_kernel(sibling, tiles, scal, ctx, part, w_ref, *rest):
    outs, (w_buf, sem) = rest[: len(tiles)], rest[len(tiles) :]
    copies = weight_tiles(scal, w_ref, w_buf, sem, sibling, tiles)
    for n, copy in enumerate(copies):
        copy.wait()
        outs[n][...] = (part[n] + dot_f32(ctx[...], w_buf[n], ((1,), (0,)))).astype(outs[n].dtype)


def both_parts_kernel(tiles, scal, ctx, ctx_sib, w_ref, *rest):
    outs, (w_own, w_sib, sem_own, sem_sib) = rest[: len(tiles)], rest[len(tiles) :]
    own = weight_tiles(scal, w_ref, w_own, sem_own, False, tiles)
    sib = weight_tiles(scal, w_ref, w_sib, sem_sib, True, tiles)
    for n in range(len(tiles)):
        own[n].wait()
        part = dot_f32(ctx[...], w_own[n], ((1,), (0,)))
        sib[n].wait()
        outs[n][...] = (part + dot_f32(ctx_sib[...], w_sib[n], ((1,), (0,)))).astype(outs[n].dtype)


def spec(space):
    return pl.BlockSpec(memory_space=space)


def call(
    kernel, name, outs, args, spaces, scratch=(), out_spaces=None, flops=0, moved=0, vmem_bytes=VMEM_BYTES
):
    return pl.pallas_call(
        kernel,
        out_shape=outs,
        in_specs=[spec(s) for s in spaces],
        out_specs=[spec(s) for s in (out_spaces or [pltpu.VMEM] * len(outs))],
        scratch_shapes=list(scratch),
        compiler_params=pltpu.CompilerParams(vmem_limit_bytes=vmem_bytes),
        cost_estimate=pl.CostEstimate(flops=flops, bytes_accessed=moved, transcendentals=0),
        name=name,
    )(*args)


def shape(dims, dtype):
    return jax.ShapeDtypeStruct(dims, dtype)


def local(queries, key_states, value_states, vert_blocks, window_size, slash_offsets, out_weight):
    smem, vmem, anywhere = pltpu.SMEM, pltpu.VMEM, pl.ANY
    place = lax.axis_index("seq").astype(I32)
    me = lax.axis_index("tp").astype(I32)
    core = place % 2
    scal = jnp.stack([core, place, me])
    block = shape((1, BLK, 2 * HD), BF16)

    k_sib = swap_cores(key_states)
    v_sib = swap_cores(value_states)
    q_sib = swap_cores(queries)
    unit, tail = call(
        pick_kernel, "pick", [shape((2, BLK, 2 * HD), BF16), shape((BLK, 2 * HD), BF16)],
        (scal, vert_blocks, key_states, value_states, k_sib, v_sib),
        [smem] + [anywhere] * 5,
        [
            pltpu.VMEM((4,) + key_states.shape, BF16),
            pltpu.SMEM(vert_blocks.shape, I32),
            pltpu.SemaphoreType.DMA((5,)),
        ],
        moved=1_000_000,
        vmem_bytes=60 * 1024 * 1024,
    )

    halo = lax.ppermute(tail, "seq", [(i, i + 2) for i in range(2 * NX * NZ - 2)])

    up1, down1 = up(unit, 0), down(unit, (1,))
    opposite = along_x(unit, 2, 0)
    up1, halo = lax.optimization_barrier((up1, halo))
    up2 = up(jnp.concatenate([up1, opposite], axis=0), 0)
    down2 = down(jnp.concatenate([down1, opposite], axis=0), (2, 1))
    up3, down3 = up(up2, 1), down(down2, (3, 2))
    first = jnp.concatenate([unit, up1, up2[:2], down1], axis=0)
    right1, left1 = along_x(first, 1, 0), along_x(first, -1, 0)

    rows = 2 * queries.shape[0]
    wide = (GROUP, rows, 2 * HD)
    qa, acc, lists, counts = call(
        local_kernel,
        "near_part",
        [shape(wide, BF16), shape(wide, F32), shape((16 * PICKS,), I32), shape((16,), I32)],
        (
            scal, vert_blocks, window_size, slash_offsets, jnp.asarray(slot_table()), queries, q_sib, key_states, k_sib, value_states, v_sib, halo,
        ),
        [smem] * 5 + [anywhere] * 7,
        [
            pltpu.VMEM((2,) + queries.shape, BF16),
            pltpu.VMEM((4,) + key_states.shape, BF16),
            pltpu.VMEM((BLK, 2 * HD), BF16),
            pltpu.VMEM((GROUP, rows, HD), BF16),
            pltpu.VMEM((rows + BLK, HD), BF16),
            pltpu.VMEM((rows + BLK, HD), BF16),
            pltpu.SMEM((GROUP * 8,), I32),
            pltpu.SemaphoreType.DMA((7,)),
        ],
        [vmem, vmem, smem, smem],
        flops=5_000_000_000,
        moved=100_000,
    )

    def far(n, pieces, qa, acc):
        sizes = [p.shape[0] for p in pieces]
        scratch = [
            pltpu.VMEM((sum(sizes) + 1, BLK, 2 * HD), BF16),
            pltpu.VMEM((2, BLK, HD), BF16),
            pltpu.SMEM((3 * (GROUP * PICKS + AT_ONCE),), I32),
            pltpu.SemaphoreType.DMA((len(sizes),)),
        ]
        final = n == 2
        outs = [shape(wide, BF16), shape(wide, F32)]
        if final:
            scratch = [pltpu.VMEM(wide, BF16), pltpu.VMEM(wide, F32)] + scratch
            outs = [shape((rows // 2, GROUP * HD), BF16)] * 2
        return call(
            functools.partial(far_kernel, n, sizes, final),
            "far_part",
            outs,
            (scal, lists, counts, qa, acc, *pieces),
            [smem] * 3 + [vmem] * 2 + [anywhere] * len(sizes),
            scratch,
            flops=6_000_000_000,
            moved=100_000,
        )

    up4 = up(up3, 2)
    second = jnp.concatenate([up3[:2], up4[:2], down2[:2], down3[:2]], axis=0)
    crossed = call(
        crossed_kernel, "crossed", [shape((8, HD), F32)], (right1, left1), [anywhere] * 2,
        flops=6_000_000_000,
    )[0]
    second, acc, crossed = lax.optimization_barrier((second, acc, crossed))
    right2, left2 = along_x(second, 1, 3), along_x(second, -1, 3)
    qa, acc = far(0, [first, right1, left1, opposite], qa, acc)
    up4, down3, acc = lax.optimization_barrier((up4, down3, acc))
    up5, down4 = up(up4[2:], 3), down(down3[2:], (3,))
    qa, acc = far(1, [right2, left2], qa, acc)
    ctx_mine, ctx_other = far(2, [up2, up3, up4, up5, down2, down3, down4], qa, acc)
    ctx_sib = swap_cores(ctx_other)

    half_rows, half = rows // 2, out_weight.shape[1] // 8
    depth = GROUP * HD

    def w_scratch(count):
        return [pltpu.VMEM((count, depth, half), BF16)], [pltpu.SemaphoreType.DMA((count,))]

    tile_bf, tile_f = shape((half_rows, half), BF16), shape((half_rows, half), F32)

    def own_part(tiles):
        return call(
            functools.partial(part_kernel, False, tiles), "own_part",
            [shape((len(tiles), half_rows, half), F32)],
            (scal, ctx_mine, out_weight), [smem, vmem, anywhere],
            sum(w_scratch(len(tiles)), []), flops=1_000_000, moved=1_000,
        )[0]

    def sib_part(tiles, part):
        return call(
            functools.partial(add_part_kernel, True, tiles), "sib_part", [tile_bf] * 2,
            (scal, ctx_sib, part, out_weight), [smem, vmem, vmem, anywhere],
            sum(w_scratch(2), []), flops=1_000_000, moved=1_000,
        )

    opp0, opp1 = sib_part((0, 1), own_part((0, 1)))
    via_before = tp_shift(opp0, 1)
    via_after = tp_shift(opp1, -1)
    after1, before0 = sib_part((3, 4), own_part((3, 4)))
    direct1 = tp_shift(after1, 1)
    direct0 = tp_shift(before0, -1)
    bufs, sems = w_scratch(4)
    after0, before1, own0, own1 = call(
        functools.partial(both_parts_kernel, (2, 5, 6, 7)), "other_shares", [tile_f] * 4,
        (scal, ctx_mine, ctx_sib, out_weight), [smem, vmem, vmem, anywhere],
        bufs * 2 + sems * 2, flops=1_000_000, moved=1_000,
    )
    summed0 = tp_shift((after0 + via_before.astype(F32)).astype(BF16), 1)
    summed1 = tp_shift((before1 + via_after.astype(F32)).astype(BF16), -1)
    return jnp.concatenate(
        [
            own0 + direct0.astype(F32) + summed0.astype(F32),
            own1 + direct1.astype(F32) + summed1.astype(F32),
        ],
        axis=1,
    ).astype(BF16)


def solution(mesh):
    return jax.shard_map(
        local,
        mesh=mesh,
        in_specs=(
            P("seq", "tp"),
            P("seq", "tp"),
            P("seq", "tp"),
            P("tp", None),
            P("tp"),
            P("tp", None),
            P("tp", None),
        ),
        out_specs=P("seq", "tp"),
        check_vma=False,
    )
```

```python
import functools
import math

import jax
import jax.numpy as jnp
import numpy as np
from jax import lax
from jax.experimental import pallas as pl
from jax.experimental.pallas import tpu as pltpu
from jax.sharding import PartitionSpec as P

HD = 128
BLK = 128
GROUP = 4
PICKS = 16
NX, NZ = 4, 8
NEG = -1e30
C2 = math.log2(math.e) / math.sqrt(HD)
LIMIT = 100.0
VMEM_BYTES = 40 * 1024 * 1024
SLOT_BITS = 6
AT_ONCE = 4
BF16, F32, I32 = jnp.bfloat16, jnp.float32, jnp.int32

STACKS = ((0, -1, -2, 1), (-3, -4, 2, 3))


def slot_table():
    table = np.zeros((NZ, NX), np.int32)

    def put(group, base, zs, dx):
        for i, dz in enumerate(zs):
            table[dz % NZ, dx % NX] = (group << SLOT_BITS) | (base + 2 * i)

    first, second = STACKS
    put(0, 0, first, 0)
    put(0, 8, first, -1)
    put(0, 16, first, 1)
    put(0, 24, (0,), 2)
    for at, dz in ((0, -3), (4, -4), (12, 2), (16, 3)):
        put(2, at, (dz,), 0)
    for at, dz in ((2, -1), (6, -2), (8, -3), (10, -4), (14, 1), (18, 2), (20, 3)):
        put(2, at, (dz,), 2)
    put(1, 0, second, -1)
    put(1, 8, second, 1)
    return table.reshape(-1)


def seq_at(z, x, core):
    return (z * NX + x) * 2 + core


def along_x(value, dx, lowest):
    pairs = [
        (seq_at(z, x, c), seq_at(z, (x + dx) % NX, c))
        for z in range(lowest, NZ)
        for x in range(NX)
        for c in range(2)
    ]
    return lax.ppermute(value, "seq", pairs)


def up(value, lowest, levels=1):
    pairs = [
        (seq_at(z, x, c), seq_at(z + levels, x, c))
        for z in range(lowest, NZ - levels)
        for x in range(NX)
        for c in range(2)
    ]
    return lax.ppermute(value, "seq", pairs)


def down(value, hops):
    steps = sorted({((s - n + 1) % NZ, (s - n) % NZ) for s in range(3) for n in hops})
    pairs = [(seq_at(a, x, c), seq_at(b, x, c)) for a, b in steps for x in range(NX) for c in range(2)]
    return lax.ppermute(value, "seq", pairs)


def swap_cores(value):
    return lax.ppermute(value, "seq", [(i, i ^ 1) for i in range(2 * NX * NZ)])


def tp_shift(value, step):
    return lax.ppermute(value, "tp", [(i, (i + step) % 4) for i in range(4)])


def dot_f32(a, b, dims):
    return lax.dot_general(a, b, (dims, ((), ())), preferred_element_type=F32)


def lanes(core, width=HD):
    return pl.ds(pl.multiple_of(core * width, width), width)


def pick_kernel(scal, blocks_ref, k_ref, v_ref, k_sib, v_sib, out_ref, tail_ref, buf, blocks, sem):
    core, place = scal[0], scal[1]
    copies = []
    for n, ref in enumerate((k_ref, v_ref, k_sib, v_sib)):
        copies.append(pltpu.make_async_copy(ref, buf.at[n], sem.at[n]))
    naming = pltpu.make_async_copy(blocks_ref, blocks, sem.at[4])
    naming.start()
    for copy in copies:
        copy.start()
    naming.wait()
    own, sib = 2 * place + 1, 2 * (place + 1 - 2 * core) + 1

    def look(n, found):
        h = n >> 4
        b = blocks[core * GROUP + h, n & 15]
        return found[0] | (b == own).astype(I32), found[1] | (b == sib).astype(I32)

    zero = jnp.int32(0)
    halves = lax.fori_loop(0, GROUP * PICKS, look, (zero, zero), unroll=8)
    for copy in copies:
        copy.wait()
    for n, parity in enumerate((core, 1 - core)):
        rows = pl.ds(pl.multiple_of(halves[n] * BLK, BLK), BLK)
        out_ref[parity, :, :HD] = buf[2 * n, rows, lanes(core)]
        out_ref[parity, :, HD:] = buf[2 * n + 1, rows, lanes(core)]
    later = 2 * (1 - core)
    tail_ref[:, :HD] = buf[later, BLK:, lanes(core)]
    tail_ref[:, HD:] = buf[later + 1, BLK:, lanes(core)]


def split3(m):
    a = m.astype(BF16)
    rest = m - a.astype(F32)
    b = rest.astype(BF16)
    c = (rest - b.astype(F32)).astype(BF16)
    return a, b, c


def extra_columns(m):
    rows = m.shape[0]
    lane = lax.broadcasted_iota(I32, (rows, HD), 1)
    a, b, c = (jnp.broadcast_to(-part.astype(F32), (rows, HD)) for part in split3(m))
    wide = jnp.where(lane == 0, a, jnp.where(lane == 1, b, jnp.where(lane == 2, c, 0.0)))
    return jnp.where(lane == 3, 1.0, wide).astype(BF16)


def local_kernel(
    scal, blocks, window, slash, table, q_ref, q_sib_ref, k_ref, k_sib_ref, v_ref, v_sib_ref, halo_ref,
    qa_ref, acc_ref, list_ref, count_ref, q_buf, kv_buf, halo, qs, ks, vs, named, sem,
):
    q, q_sib = q_buf.at[0], q_buf.at[1]
    k, k_sib, v, v_sib = (kv_buf.at[n] for n in range(4))
    copies = [
        pltpu.make_async_copy(source, into, sem.at[n])
        for n, (source, into) in enumerate(
            (
                (q_ref, q), (q_sib_ref, q_sib), (k_ref, k), (k_sib_ref, k_sib),
                (v_ref, v), (v_sib_ref, v_sib), (halo_ref, halo),
            )
        )
    ]
    for copy in copies:
        copy.start()
    core, place = scal[0], scal[1]
    chip = place >> 1
    z, x = chip >> 2, chip & 3

    for g in range(16):
        count_ref[g] = 0
    for n in range(GROUP * 8):
        named[n] = 0

    def note(n, carry):
        h = n >> 4
        b = blocks[core * GROUP + h, n & 15]
        entry = table[((((b >> 4) - z) & 7) << 2) + (((b >> 2) - x) & 3)]
        key = ((entry >> SLOT_BITS) << 2) + h
        count = count_ref[key]
        list_ref[(key << 4) + count] = (entry & ((1 << SLOT_BITS) - 1)) + ((b >> 1) & 1)
        near = b - (4 * chip - 1)
        count_ref[key] = count + jnp.where(near < 0, 1, 0)
        inside = (near >= 0) & (near < 5)
        named[(h << 3) + jnp.where(inside, near, 7)] = 1
        return carry

    lax.fori_loop(0, GROUP * PICKS, note, 0, unroll=4)

    for copy in copies:
        copy.wait()
    mine, sib = core * 2 * BLK, (1 - core) * 2 * BLK
    ks[:BLK] = halo[:, :HD]
    vs[:BLK] = halo[:, HD:]
    for ref, own, other in ((ks, k, k_sib), (vs, v, v_sib)):
        ref[pl.ds(pl.multiple_of(BLK + mine, BLK), 2 * BLK)] = own[:, lanes(core)]
        ref[pl.ds(pl.multiple_of(BLK + sib, BLK), 2 * BLK)] = other[:, lanes(core)]
    for h in range(GROUP):
        cols = pl.ds(pl.multiple_of(core * GROUP * HD + h * HD, HD), HD)
        qs[h, pl.ds(pl.multiple_of(mine, BLK), 2 * BLK)] = q[:, cols]
        qs[h, pl.ds(pl.multiple_of(sib, BLK), 2 * BLK)] = q_sib[:, cols]

    qi = lax.broadcasted_iota(I32, (BLK, BLK), 0)
    kj = lax.broadcasted_iota(I32, (BLK, BLK), 1)
    diag_gap = qi - kj
    prev_gap = diag_gap + BLK
    for h in range(GROUP):
        head = core * GROUP + h
        diag_ok = diag_gap < window[head]
        prev_ok = prev_gap < window[head]
        for n in range(8):
            diag_ok = diag_ok | (diag_gap == slash[head, n])
            prev_ok = prev_ok | (prev_gap == slash[head, n])
        scores = dot_f32(qs[h], ks[...], ((1,), (1,)))
        weights = []
        for i in range(4):
            rows = slice(i * BLK, (i + 1) * BLK)
            tiles = []
            for t in range(i + 2):
                is_named = named[h * 8 + t] > 0
                if t == i + 1:
                    ok = (diag_gap >= 0) & (diag_ok | is_named)
                elif t == i:
                    ok = prev_ok | is_named
                else:
                    ok = jnp.broadcast_to(is_named, (BLK, BLK))
                if t == 0:
                    ok = ok & (chip > 0)
                tiles.append(jnp.where(ok, scores[rows, t * BLK : (t + 1) * BLK], NEG))
            m = jnp.max(functools.reduce(jnp.maximum, tiles), axis=1, keepdims=True)
            tiles = [jnp.exp2((tile - m) * C2) for tile in tiles]
            total = jnp.sum(functools.reduce(jnp.add, tiles), axis=1, keepdims=True)
            acc_ref[h, rows, HD:] = jnp.broadcast_to(total, (BLK, HD))
            qa_ref[h, rows, :HD] = qs[h, rows, :]
            qa_ref[h, rows, HD:] = extra_columns(m)
            tiles += [jnp.zeros((BLK, BLK), F32)] * (3 - i)
            weights.append(jnp.concatenate([tile.astype(BF16) for tile in tiles], axis=1))
        acc_ref[h, :, :HD] = dot_f32(jnp.concatenate(weights, axis=0), vs[...], ((1,), (0,)))


def far_kernel(group, sizes, final, scal, lists, counts, qa_in, acc_in, *rest):
    pieces = rest[: len(sizes)]
    if final:
        mine_ref, other_ref, qa_ref, acc_ref, kv, aug, todo, sem = rest[len(sizes) :]
    else:
        qa_ref, acc_ref, kv, aug, todo, sem = rest[len(sizes) :]
    copies = []
    spare = 0
    for n, (piece, size) in enumerate(zip(pieces, sizes)):
        copies.append(pltpu.make_async_copy(piece, kv.at[pl.ds(spare, size)], sem.at[n]))
        spare += size
    for copy in copies:
        copy.start()
    kv[spare] = jnp.zeros((BLK, 2 * HD), BF16)
    lane = lax.broadcasted_iota(I32, (BLK, HD), 1)
    aug[0] = jnp.where(lane < 3, 1.0, jnp.where(lane == 3, NEG, 0.0)).astype(BF16)
    aug[1] = jnp.where(lane < 3, 1.0, 0.0).astype(BF16)
    qa_ref[...] = qa_in[...]
    acc_ref[...] = acc_in[...]

    total = jnp.int32(0)
    for h in range(GROUP):
        base = (group * GROUP + h) * PICKS
        count = counts[group * GROUP + h]

        def note(j, at, h=h, base=base, count=count):
            todo[3 * at] = h
            todo[3 * at + 1] = lists[base + 2 * j]
            more = 2 * j + 1 < count
            todo[3 * at + 2] = jnp.where(more, lists[base + 2 * j + jnp.where(more, 1, 0)], spare)
            return at + 1

        total = lax.fori_loop(0, (count + 1) >> 1, note, total)
    for n in range(AT_ONCE - 1):
        todo[3 * (total + n)] = n
        todo[3 * (total + n) + 1] = spare
        todo[3 * (total + n) + 2] = spare
    steps = (total + AT_ONCE - 1) // AT_ONCE
    for copy in copies:
        copy.wait()

    def entries(i):
        first = 3 * AT_ONCE * i
        return [tuple(todo[first + 3 * n + k] for k in range(3)) for n in range(AT_ONCE)]

    def scores(h, one, two):
        keys = jnp.concatenate([kv[one, :, :HD], kv[two, :, :HD]], axis=0)
        real = [jnp.where(slot == spare, 0, 1) for slot in (one, two)]
        more = jnp.concatenate([aug[real[0]], aug[real[1]]], axis=0)
        return dot_f32(qa_ref[h], jnp.concatenate([keys, more], axis=1), ((1,), (1,)))

    ones = jnp.ones((2 * BLK, HD), BF16)

    def accumulate():
        def step(i, high):
            work = entries(i)
            for h, one, two in work:
                s = scores(h, one, two) * C2
                values = jnp.concatenate([kv[one, :, HD:], kv[two, :, HD:]], axis=0)
                acc_ref[h] += dot_f32(
                    jnp.exp2(s).astype(BF16), jnp.concatenate([values, ones], axis=1), ((1,), (0,))
                )
                high = jnp.maximum(high, jnp.max(s.reshape(-1, 8, 2 * BLK), axis=0))
            return high

        return jnp.max(lax.fori_loop(0, steps, step, jnp.zeros((8, 2 * BLK), F32)))

    highest = accumulate()

    @pl.when(highest > LIMIT)
    def _():
        rows = qa_ref.shape[1]
        for h in range(GROUP):

            def step(n, gain, h=h):
                mine = todo[3 * n] == h
                s = scores(todo[3 * n], todo[3 * n + 1], todo[3 * n + 2])
                top = jnp.max(s, axis=1, keepdims=True)
                return jnp.maximum(gain, jnp.where(mine, top, 0.0))

            gain = lax.fori_loop(0, total, step, jnp.zeros((rows, 1), F32))
            parts = qa_ref[h, :, HD:].astype(F32)
            old = -(parts[:, 0:1] + parts[:, 1:2] + parts[:, 2:3])
            new = old + gain
            qa_ref[h, :, HD:] = extra_columns(new)
            acc_ref[h] = acc_in[h] * jnp.exp2((old - new) * C2)
        accumulate()

    if final:
        core = scal[0]
        for out, first in ((other_ref, (1 - core) * 2 * BLK), (mine_ref, core * 2 * BLK)):
            rows = pl.ds(pl.multiple_of(first, BLK), 2 * BLK)
            for h in range(GROUP):
                both = acc_ref[h, rows, :]
                out[:, h * HD : (h + 1) * HD] = (both[:, :HD] / both[:, HD:]).astype(BF16)


def crossed_kernel(right, left, out_ref):
    out_ref[...] = jnp.zeros_like(out_ref)


def weight_tiles(scal, w_ref, w_buf, sem, sibling, rel_tiles):
    core, me = scal[0], scal[2]
    rows, cols = w_buf.shape[1:]
    first = jnp.where(core == (1 if sibling else 0), 0, rows)
    copies = []
    for n, tile in enumerate(rel_tiles):
        step = (2, 1, 3, 0)[tile // 2]
        col = ((me + step) % 4) * (2 * cols) + (tile % 2) * cols
        copies.append(
            pltpu.make_async_copy(
                w_ref.at[pl.ds(pl.multiple_of(first, rows), rows), pl.ds(pl.multiple_of(col, cols), cols)],
                w_buf.at[n],
                sem.at[n],
            )
        )
    for copy in copies:
        copy.start()
    return copies


def part_kernel(sibling, tiles, scal, ctx, w_ref, out_ref, w_buf, sem):
    copies = weight_tiles(scal, w_ref, w_buf, sem, sibling, tiles)
    for n, copy in enumerate(copies):
        copy.wait()
        out_ref[n] = dot_f32(ctx[...], w_buf[n], ((1,), (0,)))


def add_part_kernel(sibling, tiles, scal, ctx, part, w_ref, *rest):
    outs, (w_buf, sem) = rest[: len(tiles)], rest[len(tiles) :]
    copies = weight_tiles(scal, w_ref, w_buf, sem, sibling, tiles)
    for n, copy in enumerate(copies):
        copy.wait()
        outs[n][...] = (part[n] + dot_f32(ctx[...], w_buf[n], ((1,), (0,)))).astype(outs[n].dtype)


def both_parts_kernel(tiles, scal, ctx, ctx_sib, w_ref, *rest):
    outs, (w_own, w_sib, sem_own, sem_sib) = rest[: len(tiles)], rest[len(tiles) :]
    own = weight_tiles(scal, w_ref, w_own, sem_own, False, tiles)
    sib = weight_tiles(scal, w_ref, w_sib, sem_sib, True, tiles)
    for n in range(len(tiles)):
        own[n].wait()
        part = dot_f32(ctx[...], w_own[n], ((1,), (0,)))
        sib[n].wait()
        outs[n][...] = (part + dot_f32(ctx_sib[...], w_sib[n], ((1,), (0,)))).astype(outs[n].dtype)


def spec(space):
    return pl.BlockSpec(memory_space=space)


def call(
    kernel, name, outs, args, spaces, scratch=(), out_spaces=None, flops=0, moved=0, vmem_bytes=VMEM_BYTES
):
    return pl.pallas_call(
        kernel,
        out_shape=outs,
        in_specs=[spec(s) for s in spaces],
        out_specs=[spec(s) for s in (out_spaces or [pltpu.VMEM] * len(outs))],
        scratch_shapes=list(scratch),
        compiler_params=pltpu.CompilerParams(vmem_limit_bytes=vmem_bytes),
        cost_estimate=pl.CostEstimate(flops=flops, bytes_accessed=moved, transcendentals=0),
        name=name,
    )(*args)


def shape(dims, dtype):
    return jax.ShapeDtypeStruct(dims, dtype)


def local(queries, key_states, value_states, vert_blocks, window_size, slash_offsets, out_weight):
    smem, vmem, anywhere = pltpu.SMEM, pltpu.VMEM, pl.ANY
    place = lax.axis_index("seq").astype(I32)
    me = lax.axis_index("tp").astype(I32)
    core = place % 2
    scal = jnp.stack([core, place, me])
    block = shape((1, BLK, 2 * HD), BF16)

    k_sib = swap_cores(key_states)
    v_sib = swap_cores(value_states)
    q_sib = swap_cores(queries)
    unit, tail = call(
        pick_kernel, "pick", [shape((2, BLK, 2 * HD), BF16), shape((BLK, 2 * HD), BF16)],
        (scal, vert_blocks, key_states, value_states, k_sib, v_sib),
        [smem] + [anywhere] * 5,
        [
            pltpu.VMEM((4,) + key_states.shape, BF16),
            pltpu.SMEM(vert_blocks.shape, I32),
            pltpu.SemaphoreType.DMA((5,)),
        ],
        moved=1_000_000,
        vmem_bytes=60 * 1024 * 1024,
    )

    halo = lax.ppermute(tail, "seq", [(i, i + 2) for i in range(2 * NX * NZ - 2)])

    up1, up2, down1 = up(unit, 0), up(unit, 0, 2), down(unit, (1,))
    opposite = along_x(unit, 2, 0)
    up2, halo = lax.optimization_barrier((up2, halo))
    up3 = up(jnp.concatenate([up2, opposite], axis=0), 0)
    down2 = down(jnp.concatenate([down1, opposite], axis=0), (2, 1))
    down3 = down(down2, (3, 2))
    first = jnp.concatenate([unit, up1, up2, down1], axis=0)
    right1, left1 = along_x(first, 1, 0), along_x(first, -1, 0)

    rows = 2 * queries.shape[0]
    wide = (GROUP, rows, 2 * HD)
    qa, acc, lists, counts = call(
        local_kernel,
        "near_part",
        [shape(wide, BF16), shape(wide, F32), shape((16 * PICKS,), I32), shape((16,), I32)],
        (
            scal, vert_blocks, window_size, slash_offsets, jnp.asarray(slot_table()), queries, q_sib, key_states, k_sib, value_states, v_sib, halo,
        ),
        [smem] * 5 + [anywhere] * 7,
        [
            pltpu.VMEM((2,) + queries.shape, BF16),
            pltpu.VMEM((4,) + key_states.shape, BF16),
            pltpu.VMEM((BLK, 2 * HD), BF16),
            pltpu.VMEM((GROUP, rows, HD), BF16),
            pltpu.VMEM((rows + BLK, HD), BF16),
            pltpu.VMEM((rows + BLK, HD), BF16),
            pltpu.SMEM((GROUP * 8,), I32),
            pltpu.SemaphoreType.DMA((7,)),
        ],
        [vmem, vmem, smem, smem],
        flops=5_000_000_000,
        moved=100_000,
    )

    def far(n, pieces, qa, acc):
        sizes = [p.shape[0] for p in pieces]
        scratch = [
            pltpu.VMEM((sum(sizes) + 1, BLK, 2 * HD), BF16),
            pltpu.VMEM((2, BLK, HD), BF16),
            pltpu.SMEM((3 * (GROUP * PICKS + AT_ONCE),), I32),
            pltpu.SemaphoreType.DMA((len(sizes),)),
        ]
        final = n == 2
        outs = [shape(wide, BF16), shape(wide, F32)]
        if final:
            scratch = [pltpu.VMEM(wide, BF16), pltpu.VMEM(wide, F32)] + scratch
            outs = [shape((rows // 2, GROUP * HD), BF16)] * 2
        return call(
            functools.partial(far_kernel, n, sizes, final),
            "far_part",
            outs,
            (scal, lists, counts, qa, acc, *pieces),
            [smem] * 3 + [vmem] * 2 + [anywhere] * len(sizes),
            scratch,
            flops=6_000_000_000,
            moved=100_000,
        )

    up4 = up(up3, 1)
    second = jnp.concatenate([up3[:2], up4[:2], down2[:2], down3[:2]], axis=0)
    crossed = call(
        crossed_kernel, "crossed", [shape((8, HD), F32)], (right1, left1), [anywhere] * 2,
        flops=6_000_000_000,
    )[0]
    second, acc, crossed = lax.optimization_barrier((second, acc, crossed))
    right2, left2 = along_x(second, 1, 3), along_x(second, -1, 3)
    qa, acc = far(0, [first, right1, left1, opposite], qa, acc)
    down3, acc = lax.optimization_barrier((down3, acc))
    up5 = up(jnp.concatenate([up3[2:], up4[2:]], axis=0), 1, 2)
    down4 = down(down3[2:], (3,))
    qa, acc = far(1, [right2, left2], qa, acc)
    ctx_mine, ctx_other = far(2, [up3, up4, up5, down2, down3, down4], qa, acc)
    ctx_sib = swap_cores(ctx_other)

    half_rows, half = rows // 2, out_weight.shape[1] // 8
    depth = GROUP * HD

    def w_scratch(count):
        return [pltpu.VMEM((count, depth, half), BF16)], [pltpu.SemaphoreType.DMA((count,))]

    tile_bf, tile_f = shape((half_rows, half), BF16), shape((half_rows, half), F32)

    def own_part(tiles):
        return call(
            functools.partial(part_kernel, False, tiles), "own_part",
            [shape((len(tiles), half_rows, half), F32)],
            (scal, ctx_mine, out_weight), [smem, vmem, anywhere],
            sum(w_scratch(len(tiles)), []), flops=1_000_000, moved=1_000,
        )[0]

    def sib_part(tiles, part):
        return call(
            functools.partial(add_part_kernel, True, tiles), "sib_part", [tile_bf] * 2,
            (scal, ctx_sib, part, out_weight), [smem, vmem, vmem, anywhere],
            sum(w_scratch(2), []), flops=1_000_000, moved=1_000,
        )

    opp0, opp1 = sib_part((0, 1), own_part((0, 1)))
    via_before = tp_shift(opp0, 1)
    via_after = tp_shift(opp1, -1)
    after1, before0 = sib_part((3, 4), own_part((3, 4)))
    direct1 = tp_shift(after1, 1)
    direct0 = tp_shift(before0, -1)
    bufs, sems = w_scratch(4)
    after0, before1, own0, own1 = call(
        functools.partial(both_parts_kernel, (2, 5, 6, 7)), "other_shares", [tile_f] * 4,
        (scal, ctx_mine, ctx_sib, out_weight), [smem, vmem, vmem, anywhere],
        bufs * 2 + sems * 2, flops=1_000_000, moved=1_000,
    )
    summed0 = tp_shift((after0 + via_before.astype(F32)).astype(BF16), 1)
    summed1 = tp_shift((before1 + via_after.astype(F32)).astype(BF16), -1)
    return jnp.concatenate(
        [
            own0 + direct0.astype(F32) + summed0.astype(F32),
            own1 + direct1.astype(F32) + summed1.astype(F32),
        ],
        axis=1,
    ).astype(BF16)


def solution(mesh):
    return jax.shard_map(
        local,
        mesh=mesh,
        in_specs=(
            P("seq", "tp"),
            P("seq", "tp"),
            P("seq", "tp"),
            P("tp", None),
            P("tp"),
            P("tp", None),
            P("tp", None),
        ),
        out_specs=P("seq", "tp"),
        check_vma=False,
    )
```

```python
import functools
import math

import jax
import jax.numpy as jnp
import numpy as np
from jax import lax
from jax.experimental import pallas as pl
from jax.experimental.pallas import tpu as pltpu
from jax.sharding import PartitionSpec as P

HD = 128
BLK = 128
GROUP = 4
PICKS = 16
NX, NZ = 4, 8
NEG = -1e30
C2 = math.log2(math.e) / math.sqrt(HD)
LIMIT = 100.0
VMEM_BYTES = 40 * 1024 * 1024
SLOT_BITS = 6
AT_ONCE = 4
BF16, F32, I32 = jnp.bfloat16, jnp.float32, jnp.int32

STACKS = ((0, -1, -2, 1), (-3, -4, 2, 3))


def slot_table():
    table = np.zeros((NZ, NX), np.int32)

    def put(group, base, zs, dx):
        for i, dz in enumerate(zs):
            table[dz % NZ, dx % NX] = (group << SLOT_BITS) | (base + 2 * i)

    first, second = STACKS
    put(0, 0, first, 0)
    put(0, 8, first, -1)
    put(0, 16, first, 1)
    put(0, 24, (0,), 2)
    for at, dz in ((26, -3), (30, -4), (34, 2), (38, 3)):
        put(0, at, (dz,), 0)
    for at, dz in ((28, -1), (32, -2), (36, 1), (40, 2)):
        put(0, at, (dz,), 2)
    put(1, 16, (-3, -4, 3), 2)
    put(1, 0, second, -1)
    put(1, 8, second, 1)
    return table.reshape(-1)


def seq_at(z, x, core):
    return (z * NX + x) * 2 + core


def along_x(value, dx, lowest):
    pairs = [
        (seq_at(z, x, c), seq_at(z, (x + dx) % NX, c))
        for z in range(lowest, NZ)
        for x in range(NX)
        for c in range(2)
    ]
    return lax.ppermute(value, "seq", pairs)


def up(value, lowest, levels=1):
    pairs = [
        (seq_at(z, x, c), seq_at(z + levels, x, c))
        for z in range(lowest, NZ - levels)
        for x in range(NX)
        for c in range(2)
    ]
    return lax.ppermute(value, "seq", pairs)


def down(value, hops):
    steps = sorted({((s - n + 1) % NZ, (s - n) % NZ) for s in range(3) for n in hops})
    pairs = [(seq_at(a, x, c), seq_at(b, x, c)) for a, b in steps for x in range(NX) for c in range(2)]
    return lax.ppermute(value, "seq", pairs)


def swap_cores(value):
    return lax.ppermute(value, "seq", [(i, i ^ 1) for i in range(2 * NX * NZ)])


def tp_shift(value, step):
    return lax.ppermute(value, "tp", [(i, (i + step) % 4) for i in range(4)])


def dot_f32(a, b, dims):
    return lax.dot_general(a, b, (dims, ((), ())), preferred_element_type=F32)


def lanes(core, width=HD):
    return pl.ds(pl.multiple_of(core * width, width), width)


def pick_kernel(scal, blocks_ref, k_ref, v_ref, k_sib, v_sib, out_ref, tail_ref, buf, blocks, sem):
    core, place = scal[0], scal[1]
    copies = []
    for n, ref in enumerate((k_ref, v_ref, k_sib, v_sib)):
        copies.append(pltpu.make_async_copy(ref, buf.at[n], sem.at[n]))
    naming = pltpu.make_async_copy(blocks_ref, blocks, sem.at[4])
    naming.start()
    for copy in copies:
        copy.start()
    naming.wait()
    own, sib = 2 * place + 1, 2 * (place + 1 - 2 * core) + 1

    def look(n, found):
        h = n >> 4
        b = blocks[core * GROUP + h, n & 15]
        return found[0] | (b == own).astype(I32), found[1] | (b == sib).astype(I32)

    zero = jnp.int32(0)
    halves = lax.fori_loop(0, GROUP * PICKS, look, (zero, zero), unroll=8)
    for copy in copies:
        copy.wait()
    for n, parity in enumerate((core, 1 - core)):
        rows = pl.ds(pl.multiple_of(halves[n] * BLK, BLK), BLK)
        out_ref[parity, :, :HD] = buf[2 * n, rows, lanes(core)]
        out_ref[parity, :, HD:] = buf[2 * n + 1, rows, lanes(core)]
    later = 2 * (1 - core)
    tail_ref[:, :HD] = buf[later, BLK:, lanes(core)]
    tail_ref[:, HD:] = buf[later + 1, BLK:, lanes(core)]


def split3(m):
    a = m.astype(BF16)
    rest = m - a.astype(F32)
    b = rest.astype(BF16)
    c = (rest - b.astype(F32)).astype(BF16)
    return a, b, c


def extra_columns(m):
    rows = m.shape[0]
    lane = lax.broadcasted_iota(I32, (rows, HD), 1)
    a, b, c = (jnp.broadcast_to(-part.astype(F32), (rows, HD)) for part in split3(m))
    wide = jnp.where(lane == 0, a, jnp.where(lane == 1, b, jnp.where(lane == 2, c, 0.0)))
    return jnp.where(lane == 3, 1.0, wide).astype(BF16)


def local_kernel(
    scal, blocks, window, slash, table, q_ref, q_sib_ref, k_ref, k_sib_ref, v_ref, v_sib_ref, halo_ref,
    qa_ref, acc_ref, list_ref, count_ref, q_buf, kv_buf, halo, qs, ks, vs, named, sem,
):
    q, q_sib = q_buf.at[0], q_buf.at[1]
    k, k_sib, v, v_sib = (kv_buf.at[n] for n in range(4))
    copies = [
        pltpu.make_async_copy(source, into, sem.at[n])
        for n, (source, into) in enumerate(
            (
                (q_ref, q), (q_sib_ref, q_sib), (k_ref, k), (k_sib_ref, k_sib),
                (v_ref, v), (v_sib_ref, v_sib), (halo_ref, halo),
            )
        )
    ]
    for copy in copies:
        copy.start()
    core, place = scal[0], scal[1]
    chip = place >> 1
    z, x = chip >> 2, chip & 3

    for g in range(16):
        count_ref[g] = 0
    for n in range(GROUP * 8):
        named[n] = 0

    def note(n, carry):
        h = n >> 4
        b = blocks[core * GROUP + h, n & 15]
        entry = table[((((b >> 4) - z) & 7) << 2) + (((b >> 2) - x) & 3)]
        key = ((entry >> SLOT_BITS) << 2) + h
        count = count_ref[key]
        list_ref[(key << 4) + count] = (entry & ((1 << SLOT_BITS) - 1)) + ((b >> 1) & 1)
        near = b - (4 * chip - 1)
        count_ref[key] = count + jnp.where(near < 0, 1, 0)
        inside = (near >= 0) & (near < 5)
        named[(h << 3) + jnp.where(inside, near, 7)] = 1
        return carry

    lax.fori_loop(0, GROUP * PICKS, note, 0, unroll=4)

    for copy in copies:
        copy.wait()
    mine, sib = core * 2 * BLK, (1 - core) * 2 * BLK
    ks[:BLK] = halo[:, :HD]
    vs[:BLK] = halo[:, HD:]
    for ref, own, other in ((ks, k, k_sib), (vs, v, v_sib)):
        ref[pl.ds(pl.multiple_of(BLK + mine, BLK), 2 * BLK)] = own[:, lanes(core)]
        ref[pl.ds(pl.multiple_of(BLK + sib, BLK), 2 * BLK)] = other[:, lanes(core)]
    for h in range(GROUP):
        cols = pl.ds(pl.multiple_of(core * GROUP * HD + h * HD, HD), HD)
        qs[h, pl.ds(pl.multiple_of(mine, BLK), 2 * BLK)] = q[:, cols]
        qs[h, pl.ds(pl.multiple_of(sib, BLK), 2 * BLK)] = q_sib[:, cols]

    qi = lax.broadcasted_iota(I32, (BLK, BLK), 0)
    kj = lax.broadcasted_iota(I32, (BLK, BLK), 1)
    diag_gap = qi - kj
    prev_gap = diag_gap + BLK
    for h in range(GROUP):
        head = core * GROUP + h
        diag_ok = diag_gap < window[head]
        prev_ok = prev_gap < window[head]
        for n in range(8):
            diag_ok = diag_ok | (diag_gap == slash[head, n])
            prev_ok = prev_ok | (prev_gap == slash[head, n])
        scores = dot_f32(qs[h], ks[...], ((1,), (1,)))
        weights = []
        for i in range(4):
            rows = slice(i * BLK, (i + 1) * BLK)
            tiles = []
            for t in range(i + 2):
                is_named = named[h * 8 + t] > 0
                if t == i + 1:
                    ok = (diag_gap >= 0) & (diag_ok | is_named)
                elif t == i:
                    ok = prev_ok | is_named
                else:
                    ok = jnp.broadcast_to(is_named, (BLK, BLK))
                if t == 0:
                    ok = ok & (chip > 0)
                tiles.append(jnp.where(ok, scores[rows, t * BLK : (t + 1) * BLK], NEG))
            m = jnp.max(functools.reduce(jnp.maximum, tiles), axis=1, keepdims=True)
            tiles = [jnp.exp2((tile - m) * C2) for tile in tiles]
            total = jnp.sum(functools.reduce(jnp.add, tiles), axis=1, keepdims=True)
            acc_ref[h, rows, HD:] = jnp.broadcast_to(total, (BLK, HD))
            qa_ref[h, rows, :HD] = qs[h, rows, :]
            qa_ref[h, rows, HD:] = extra_columns(m)
            tiles += [jnp.zeros((BLK, BLK), F32)] * (3 - i)
            weights.append(jnp.concatenate([tile.astype(BF16) for tile in tiles], axis=1))
        acc_ref[h, :, :HD] = dot_f32(jnp.concatenate(weights, axis=0), vs[...], ((1,), (0,)))


def far_kernel(group, sizes, final, scal, lists, counts, qa_in, acc_in, *rest):
    pieces = rest[: len(sizes)]
    if final:
        mine_ref, other_ref, qa_ref, acc_ref, kv, aug, todo, sem = rest[len(sizes) :]
    else:
        qa_ref, acc_ref, kv, aug, todo, sem = rest[len(sizes) :]
    copies = []
    spare = 0
    for n, (piece, size) in enumerate(zip(pieces, sizes)):
        copies.append(pltpu.make_async_copy(piece, kv.at[pl.ds(spare, size)], sem.at[n]))
        spare += size
    for copy in copies:
        copy.start()
    kv[spare] = jnp.zeros((BLK, 2 * HD), BF16)
    lane = lax.broadcasted_iota(I32, (BLK, HD), 1)
    aug[0] = jnp.where(lane < 3, 1.0, jnp.where(lane == 3, NEG, 0.0)).astype(BF16)
    aug[1] = jnp.where(lane < 3, 1.0, 0.0).astype(BF16)
    qa_ref[...] = qa_in[...]
    acc_ref[...] = acc_in[...]

    total = jnp.int32(0)
    for h in range(GROUP):
        base = (group * GROUP + h) * PICKS
        count = counts[group * GROUP + h]

        def note(j, at, h=h, base=base, count=count):
            todo[3 * at] = h
            todo[3 * at + 1] = lists[base + 2 * j]
            more = 2 * j + 1 < count
            todo[3 * at + 2] = jnp.where(more, lists[base + 2 * j + jnp.where(more, 1, 0)], spare)
            return at + 1

        total = lax.fori_loop(0, (count + 1) >> 1, note, total)
    for n in range(AT_ONCE - 1):
        todo[3 * (total + n)] = n
        todo[3 * (total + n) + 1] = spare
        todo[3 * (total + n) + 2] = spare
    steps = (total + AT_ONCE - 1) // AT_ONCE
    for copy in copies:
        copy.wait()

    def entries(i):
        first = 3 * AT_ONCE * i
        return [tuple(todo[first + 3 * n + k] for k in range(3)) for n in range(AT_ONCE)]

    def scores(h, one, two):
        keys = jnp.concatenate([kv[one, :, :HD], kv[two, :, :HD]], axis=0)
        real = [jnp.where(slot == spare, 0, 1) for slot in (one, two)]
        more = jnp.concatenate([aug[real[0]], aug[real[1]]], axis=0)
        return dot_f32(qa_ref[h], jnp.concatenate([keys, more], axis=1), ((1,), (1,)))

    ones = jnp.ones((2 * BLK, HD), BF16)

    def accumulate():
        def step(i, high):
            work = entries(i)
            for h, one, two in work:
                s = scores(h, one, two) * C2
                values = jnp.concatenate([kv[one, :, HD:], kv[two, :, HD:]], axis=0)
                acc_ref[h] += dot_f32(
                    jnp.exp2(s).astype(BF16), jnp.concatenate([values, ones], axis=1), ((1,), (0,))
                )
                high = jnp.maximum(high, jnp.max(s.reshape(-1, 8, 2 * BLK), axis=0))
            return high

        return jnp.max(lax.fori_loop(0, steps, step, jnp.zeros((8, 2 * BLK), F32)))

    highest = accumulate()

    @pl.when(highest > LIMIT)
    def _():
        rows = qa_ref.shape[1]
        for h in range(GROUP):

            def step(n, gain, h=h):
                mine = todo[3 * n] == h
                s = scores(todo[3 * n], todo[3 * n + 1], todo[3 * n + 2])
                top = jnp.max(s, axis=1, keepdims=True)
                return jnp.maximum(gain, jnp.where(mine, top, 0.0))

            gain = lax.fori_loop(0, total, step, jnp.zeros((rows, 1), F32))
            parts = qa_ref[h, :, HD:].astype(F32)
            old = -(parts[:, 0:1] + parts[:, 1:2] + parts[:, 2:3])
            new = old + gain
            qa_ref[h, :, HD:] = extra_columns(new)
            acc_ref[h] = acc_in[h] * jnp.exp2((old - new) * C2)
        accumulate()

    if final:
        core = scal[0]
        for out, first in ((other_ref, (1 - core) * 2 * BLK), (mine_ref, core * 2 * BLK)):
            rows = pl.ds(pl.multiple_of(first, BLK), 2 * BLK)
            for h in range(GROUP):
                both = acc_ref[h, rows, :]
                out[:, h * HD : (h + 1) * HD] = (both[:, :HD] / both[:, HD:]).astype(BF16)


def crossed_kernel(right, left, out_ref):
    out_ref[...] = jnp.zeros_like(out_ref)


def weight_tiles(scal, w_ref, w_buf, sem, sibling, rel_tiles):
    core, me = scal[0], scal[2]
    rows, cols = w_buf.shape[1:]
    first = jnp.where(core == (1 if sibling else 0), 0, rows)
    copies = []
    for n, tile in enumerate(rel_tiles):
        step = (2, 1, 3, 0)[tile // 2]
        col = ((me + step) % 4) * (2 * cols) + (tile % 2) * cols
        copies.append(
            pltpu.make_async_copy(
                w_ref.at[pl.ds(pl.multiple_of(first, rows), rows), pl.ds(pl.multiple_of(col, cols), cols)],
                w_buf.at[n],
                sem.at[n],
            )
        )
    for copy in copies:
        copy.start()
    return copies


def part_kernel(sibling, tiles, scal, ctx, w_ref, out_ref, w_buf, sem):
    copies = weight_tiles(scal, w_ref, w_buf, sem, sibling, tiles)
    for n, copy in enumerate(copies):
        copy.wait()
        out_ref[n] = dot_f32(ctx[...], w_buf[n], ((1,), (0,)))


def add_part_kernel(sibling, tiles, scal, ctx, part, w_ref, *rest):
    outs, (w_buf, sem) = rest[: len(tiles)], rest[len(tiles) :]
    copies = weight_tiles(scal, w_ref, w_buf, sem, sibling, tiles)
    for n, copy in enumerate(copies):
        copy.wait()
        outs[n][...] = (part[n] + dot_f32(ctx[...], w_buf[n], ((1,), (0,)))).astype(outs[n].dtype)


def both_parts_kernel(tiles, scal, ctx, ctx_sib, w_ref, *rest):
    outs, (w_own, w_sib, sem_own, sem_sib) = rest[: len(tiles)], rest[len(tiles) :]
    own = weight_tiles(scal, w_ref, w_own, sem_own, False, tiles)
    sib = weight_tiles(scal, w_ref, w_sib, sem_sib, True, tiles)
    for n in range(len(tiles)):
        own[n].wait()
        part = dot_f32(ctx[...], w_own[n], ((1,), (0,)))
        sib[n].wait()
        outs[n][...] = (part + dot_f32(ctx_sib[...], w_sib[n], ((1,), (0,)))).astype(outs[n].dtype)


def spec(space):
    return pl.BlockSpec(memory_space=space)


def call(
    kernel, name, outs, args, spaces, scratch=(), out_spaces=None, flops=0, moved=0, vmem_bytes=VMEM_BYTES
):
    return pl.pallas_call(
        kernel,
        out_shape=outs,
        in_specs=[spec(s) for s in spaces],
        out_specs=[spec(s) for s in (out_spaces or [pltpu.VMEM] * len(outs))],
        scratch_shapes=list(scratch),
        compiler_params=pltpu.CompilerParams(vmem_limit_bytes=vmem_bytes),
        cost_estimate=pl.CostEstimate(flops=flops, bytes_accessed=moved, transcendentals=0),
        name=name,
    )(*args)


def shape(dims, dtype):
    return jax.ShapeDtypeStruct(dims, dtype)


def local(queries, key_states, value_states, vert_blocks, window_size, slash_offsets, out_weight):
    smem, vmem, anywhere = pltpu.SMEM, pltpu.VMEM, pl.ANY
    place = lax.axis_index("seq").astype(I32)
    me = lax.axis_index("tp").astype(I32)
    core = place % 2
    scal = jnp.stack([core, place, me])
    block = shape((1, BLK, 2 * HD), BF16)

    k_sib = swap_cores(key_states)
    v_sib = swap_cores(value_states)
    q_sib = swap_cores(queries)
    unit, tail = call(
        pick_kernel, "pick", [shape((2, BLK, 2 * HD), BF16), shape((BLK, 2 * HD), BF16)],
        (scal, vert_blocks, key_states, value_states, k_sib, v_sib),
        [smem] + [anywhere] * 5,
        [
            pltpu.VMEM((4,) + key_states.shape, BF16),
            pltpu.SMEM(vert_blocks.shape, I32),
            pltpu.SemaphoreType.DMA((5,)),
        ],
        moved=1_000_000,
        vmem_bytes=60 * 1024 * 1024,
    )

    halo = lax.ppermute(tail, "seq", [(i, i + 2) for i in range(2 * NX * NZ - 2)])

    up1, up2, down1 = up(unit, 0), up(unit, 0, 2), down(unit, (1,))
    opposite = along_x(unit, 2, 0)
    up2, halo = lax.optimization_barrier((up2, halo))
    up3 = up(jnp.concatenate([up2, opposite], axis=0), 0)
    down2 = down(jnp.concatenate([down1, opposite], axis=0), (2, 1))
    down3 = down(down2, (3, 2))
    first = jnp.concatenate([unit, up1, up2, down1], axis=0)
    right1, left1 = along_x(first, 1, 0), along_x(first, -1, 0)

    rows = 2 * queries.shape[0]
    wide = (GROUP, rows, 2 * HD)
    qa, acc, lists, counts = call(
        local_kernel,
        "near_part",
        [shape(wide, BF16), shape(wide, F32), shape((16 * PICKS,), I32), shape((16,), I32)],
        (
            scal, vert_blocks, window_size, slash_offsets, jnp.asarray(slot_table()), queries, q_sib, key_states, k_sib, value_states, v_sib, halo,
        ),
        [smem] * 5 + [anywhere] * 7,
        [
            pltpu.VMEM((2,) + queries.shape, BF16),
            pltpu.VMEM((4,) + key_states.shape, BF16),
            pltpu.VMEM((BLK, 2 * HD), BF16),
            pltpu.VMEM((GROUP, rows, HD), BF16),
            pltpu.VMEM((rows + BLK, HD), BF16),
            pltpu.VMEM((rows + BLK, HD), BF16),
            pltpu.SMEM((GROUP * 8,), I32),
            pltpu.SemaphoreType.DMA((7,)),
        ],
        [vmem, vmem, smem, smem],
        flops=5_000_000_000,
        moved=100_000,
    )

    def far(n, pieces, qa, acc):
        sizes = [p.shape[0] for p in pieces]
        scratch = [
            pltpu.VMEM((sum(sizes) + 1, BLK, 2 * HD), BF16),
            pltpu.VMEM((2, BLK, HD), BF16),
            pltpu.SMEM((3 * (GROUP * PICKS + AT_ONCE),), I32),
            pltpu.SemaphoreType.DMA((len(sizes),)),
        ]
        final = n == 1
        outs = [shape(wide, BF16), shape(wide, F32)]
        if final:
            scratch = [pltpu.VMEM(wide, BF16), pltpu.VMEM(wide, F32)] + scratch
            outs = [shape((rows // 2, GROUP * HD), BF16)] * 2
        return call(
            functools.partial(far_kernel, n, sizes, final),
            "far_part",
            outs,
            (scal, lists, counts, qa, acc, *pieces),
            [smem] * 3 + [vmem] * 2 + [anywhere] * len(sizes),
            scratch,
            flops=6_000_000_000,
            moved=100_000,
        )

    up4 = up(up3, 1)
    second = jnp.concatenate([up3[:2], up4[:2], down2[:2], down3[:2]], axis=0)
    crossed = call(
        crossed_kernel, "crossed", [shape((8, HD), F32)], (right1, left1), [anywhere] * 2,
        flops=6_000_000_000,
    )[0]
    second, acc, crossed = lax.optimization_barrier((second, acc, crossed))
    right2, left2 = along_x(second, 1, 3), along_x(second, -1, 3)
    qa, acc = far(0, [first, right1, left1, opposite, up3, up4, down2, down3], qa, acc)
    up5, up6 = up(up4[2:], 2), up(up4[2:], 2, 2)
    down4 = down(down3[2:], (3,))
    ctx_mine, ctx_other = far(1, [right2, left2, up5, up6, down4], qa, acc)
    ctx_sib = swap_cores(ctx_other)

    half_rows, half = rows // 2, out_weight.shape[1] // 8
    depth = GROUP * HD

    def w_scratch(count):
        return [pltpu.VMEM((count, depth, half), BF16)], [pltpu.SemaphoreType.DMA((count,))]

    tile_bf, tile_f = shape((half_rows, half), BF16), shape((half_rows, half), F32)

    def own_part(tiles):
        return call(
            functools.partial(part_kernel, False, tiles), "own_part",
            [shape((len(tiles), half_rows, half), F32)],
            (scal, ctx_mine, out_weight), [smem, vmem, anywhere],
            sum(w_scratch(len(tiles)), []), flops=1_000_000, moved=1_000,
        )[0]

    def sib_part(tiles, part):
        return call(
            functools.partial(add_part_kernel, True, tiles), "sib_part", [tile_bf] * 2,
            (scal, ctx_sib, part, out_weight), [smem, vmem, vmem, anywhere],
            sum(w_scratch(2), []), flops=1_000_000, moved=1_000,
        )

    opp0, opp1 = sib_part((0, 1), own_part((0, 1)))
    via_before = tp_shift(opp0, 1)
    via_after = tp_shift(opp1, -1)
    after1, before0 = sib_part((3, 4), own_part((3, 4)))
    direct1 = tp_shift(after1, 1)
    direct0 = tp_shift(before0, -1)
    bufs, sems = w_scratch(4)
    after0, before1, own0, own1 = call(
        functools.partial(both_parts_kernel, (2, 5, 6, 7)), "other_shares", [tile_f] * 4,
        (scal, ctx_mine, ctx_sib, out_weight), [smem, vmem, vmem, anywhere],
        bufs * 2 + sems * 2, flops=1_000_000, moved=1_000,
    )
    summed0 = tp_shift((after0 + via_before.astype(F32)).astype(BF16), 1)
    summed1 = tp_shift((before1 + via_after.astype(F32)).astype(BF16), -1)
    return jnp.concatenate(
        [
            own0 + direct0.astype(F32) + summed0.astype(F32),
            own1 + direct1.astype(F32) + summed1.astype(F32),
        ],
        axis=1,
    ).astype(BF16)


def solution(mesh):
    return jax.shard_map(
        local,
        mesh=mesh,
        in_specs=(
            P("seq", "tp"),
            P("seq", "tp"),
            P("seq", "tp"),
            P("tp", None),
            P("tp"),
            P("tp", None),
            P("tp", None),
        ),
        out_specs=P("seq", "tp"),
        check_vma=False,
    )
```

```python
import functools
import math

import jax
import jax.numpy as jnp
import numpy as np
from jax import lax
from jax.experimental import pallas as pl
from jax.experimental.pallas import tpu as pltpu
from jax.sharding import PartitionSpec as P

HD = 128
BLK = 128
GROUP = 4
PICKS = 16
NX, NZ = 4, 8
NEG = -1e30
C2 = math.log2(math.e) / math.sqrt(HD)
LIMIT = 100.0
VMEM_BYTES = 40 * 1024 * 1024
SLOT_BITS = 6
AT_ONCE = 4
BF16, F32, I32 = jnp.bfloat16, jnp.float32, jnp.int32

STACKS = ((0, -1, -2, 1), (-3, -4, 2, 3))


def slot_table():
    table = np.zeros((NZ, NX), np.int32)

    def put(group, base, zs, dx):
        for i, dz in enumerate(zs):
            table[dz % NZ, dx % NX] = (group << SLOT_BITS) | (base + 2 * i)

    first, second = STACKS
    put(0, 0, first, 0)
    put(0, 8, first, -1)
    put(0, 16, first, 1)
    put(0, 24, (0,), 2)
    for at, dz in ((26, -3), (30, -4), (34, 2), (38, 3)):
        put(0, at, (dz,), 0)
    for at, dz in ((28, -1), (32, -2), (36, 1), (40, 2)):
        put(0, at, (dz,), 2)
    put(1, 16, (-3, -4, 3), 2)
    put(1, 0, second, -1)
    put(1, 8, second, 1)
    return table.reshape(-1)


def seq_at(z, x, core):
    return (z * NX + x) * 2 + core


def along_x(value, dx, lowest):
    pairs = [
        (seq_at(z, x, c), seq_at(z, (x + dx) % NX, c))
        for z in range(lowest, NZ)
        for x in range(NX)
        for c in range(2)
    ]
    return lax.ppermute(value, "seq", pairs)


def up(value, lowest, levels=1):
    pairs = [
        (seq_at(z, x, c), seq_at(z + levels, x, c))
        for z in range(lowest, NZ - levels)
        for x in range(NX)
        for c in range(2)
    ]
    return lax.ppermute(value, "seq", pairs)


def down(value, hops):
    steps = sorted({((s - n + 1) % NZ, (s - n) % NZ) for s in range(3) for n in hops})
    pairs = [(seq_at(a, x, c), seq_at(b, x, c)) for a, b in steps for x in range(NX) for c in range(2)]
    return lax.ppermute(value, "seq", pairs)


def swap_cores(value):
    return lax.ppermute(value, "seq", [(i, i ^ 1) for i in range(2 * NX * NZ)])


def tp_shift(value, step):
    return lax.ppermute(value, "tp", [(i, (i + step) % 4) for i in range(4)])


def dot_f32(a, b, dims):
    return lax.dot_general(a, b, (dims, ((), ())), preferred_element_type=F32)


def lanes(core, width=HD):
    return pl.ds(pl.multiple_of(core * width, width), width)


def pick_kernel(scal, blocks_ref, k_ref, v_ref, k_sib, v_sib, out_ref, tail_ref, buf, blocks, sem):
    core, place = scal[0], scal[1]
    copies = []
    for n, ref in enumerate((k_ref, v_ref, k_sib, v_sib)):
        copies.append(pltpu.make_async_copy(ref, buf.at[n], sem.at[n]))
    naming = pltpu.make_async_copy(blocks_ref, blocks, sem.at[4])
    naming.start()
    for copy in copies:
        copy.start()
    naming.wait()
    own, sib = 2 * place + 1, 2 * (place + 1 - 2 * core) + 1

    def look(n, found):
        h = n >> 4
        b = blocks[core * GROUP + h, n & 15]
        return found[0] | (b == own).astype(I32), found[1] | (b == sib).astype(I32)

    zero = jnp.int32(0)
    halves = lax.fori_loop(0, GROUP * PICKS, look, (zero, zero), unroll=8)
    for copy in copies:
        copy.wait()
    for n, parity in enumerate((core, 1 - core)):
        rows = pl.ds(pl.multiple_of(halves[n] * BLK, BLK), BLK)
        out_ref[parity, :, :HD] = buf[2 * n, rows, lanes(core)]
        out_ref[parity, :, HD:] = buf[2 * n + 1, rows, lanes(core)]
    later = 2 * (1 - core)
    tail_ref[:, :HD] = buf[later, BLK:, lanes(core)]
    tail_ref[:, HD:] = buf[later + 1, BLK:, lanes(core)]


def split3(m):
    a = m.astype(BF16)
    rest = m - a.astype(F32)
    b = rest.astype(BF16)
    c = (rest - b.astype(F32)).astype(BF16)
    return a, b, c


def extra_columns(m):
    rows = m.shape[0]
    lane = lax.broadcasted_iota(I32, (rows, HD), 1)
    a, b, c = (jnp.broadcast_to(-part.astype(F32), (rows, HD)) for part in split3(m))
    wide = jnp.where(lane == 0, a, jnp.where(lane == 1, b, jnp.where(lane == 2, c, 0.0)))
    return jnp.where(lane == 3, 1.0, wide).astype(BF16)


def local_kernel(
    scal, blocks, window, slash, table, q_ref, q_sib_ref, k_ref, k_sib_ref, v_ref, v_sib_ref, halo_ref,
    qa_ref, acc_ref, list_ref, count_ref, q_buf, kv_buf, halo, qs, ks, vs, named, sem,
):
    q, q_sib = q_buf.at[0], q_buf.at[1]
    k, k_sib, v, v_sib = (kv_buf.at[n] for n in range(4))
    copies = [
        pltpu.make_async_copy(source, into, sem.at[n])
        for n, (source, into) in enumerate(
            (
                (q_ref, q), (q_sib_ref, q_sib), (k_ref, k), (k_sib_ref, k_sib),
                (v_ref, v), (v_sib_ref, v_sib), (halo_ref, halo),
            )
        )
    ]
    for copy in copies:
        copy.start()
    core, place = scal[0], scal[1]
    chip = place >> 1
    z, x = chip >> 2, chip & 3

    for g in range(16):
        count_ref[g] = 0
    for n in range(GROUP * 8):
        named[n] = 0

    def note(n, carry):
        h = n >> 4
        b = blocks[core * GROUP + h, n & 15]
        entry = table[((((b >> 4) - z) & 7) << 2) + (((b >> 2) - x) & 3)]
        key = ((entry >> SLOT_BITS) << 2) + h
        count = count_ref[key]
        list_ref[(key << 4) + count] = (entry & ((1 << SLOT_BITS) - 1)) + ((b >> 1) & 1)
        near = b - (4 * chip - 1)
        count_ref[key] = count + jnp.where(near < 0, 1, 0)
        inside = (near >= 0) & (near < 5)
        named[(h << 3) + jnp.where(inside, near, 7)] = 1
        return carry

    lax.fori_loop(0, GROUP * PICKS, note, 0, unroll=4)

    for copy in copies:
        copy.wait()
    mine, sib = core * 2 * BLK, (1 - core) * 2 * BLK
    ks[:BLK] = halo[:, :HD]
    vs[:BLK] = halo[:, HD:]
    for ref, own, other in ((ks, k, k_sib), (vs, v, v_sib)):
        ref[pl.ds(pl.multiple_of(BLK + mine, BLK), 2 * BLK)] = own[:, lanes(core)]
        ref[pl.ds(pl.multiple_of(BLK + sib, BLK), 2 * BLK)] = other[:, lanes(core)]
    for h in range(GROUP):
        cols = pl.ds(pl.multiple_of(core * GROUP * HD + h * HD, HD), HD)
        qs[h, pl.ds(pl.multiple_of(mine, BLK), 2 * BLK)] = q[:, cols]
        qs[h, pl.ds(pl.multiple_of(sib, BLK), 2 * BLK)] = q_sib[:, cols]

    qi = lax.broadcasted_iota(I32, (BLK, BLK), 0)
    kj = lax.broadcasted_iota(I32, (BLK, BLK), 1)
    diag_gap = qi - kj
    prev_gap = diag_gap + BLK
    for h in range(GROUP):
        head = core * GROUP + h
        diag_ok = diag_gap < window[head]
        prev_ok = prev_gap < window[head]
        for n in range(8):
            diag_ok = diag_ok | (diag_gap == slash[head, n])
            prev_ok = prev_ok | (prev_gap == slash[head, n])
        scores = dot_f32(qs[h], ks[...], ((1,), (1,)))
        weights = []
        for i in range(4):
            rows = slice(i * BLK, (i + 1) * BLK)
            tiles = []
            for t in range(i + 2):
                is_named = named[h * 8 + t] > 0
                if t == i + 1:
                    ok = (diag_gap >= 0) & (diag_ok | is_named)
                elif t == i:
                    ok = prev_ok | is_named
                else:
                    ok = jnp.broadcast_to(is_named, (BLK, BLK))
                if t == 0:
                    ok = ok & (chip > 0)
                tiles.append(jnp.where(ok, scores[rows, t * BLK : (t + 1) * BLK], NEG))
            m = jnp.max(functools.reduce(jnp.maximum, tiles), axis=1, keepdims=True)
            tiles = [jnp.exp2((tile - m) * C2) for tile in tiles]
            total = jnp.sum(functools.reduce(jnp.add, tiles), axis=1, keepdims=True)
            acc_ref[h, rows, HD:] = jnp.broadcast_to(total, (BLK, HD))
            qa_ref[h, rows, :HD] = qs[h, rows, :]
            qa_ref[h, rows, HD:] = extra_columns(m)
            tiles += [jnp.zeros((BLK, BLK), F32)] * (3 - i)
            weights.append(jnp.concatenate([tile.astype(BF16) for tile in tiles], axis=1))
        acc_ref[h, :, :HD] = dot_f32(jnp.concatenate(weights, axis=0), vs[...], ((1,), (0,)))


def far_kernel(group, sizes, final, scal, lists, counts, qa_in, acc_in, *rest):
    pieces = rest[: len(sizes)]
    if final:
        mine_ref, other_ref, qa_ref, acc_ref, kv, aug, todo, sem = rest[len(sizes) :]
    else:
        qa_ref, acc_ref, kv, aug, todo, sem = rest[len(sizes) :]
    copies = []
    spare = 0
    for n, (piece, size) in enumerate(zip(pieces, sizes)):
        copies.append(pltpu.make_async_copy(piece, kv.at[pl.ds(spare, size)], sem.at[n]))
        spare += size
    for copy in copies:
        copy.start()
    kv[spare] = jnp.zeros((BLK, 2 * HD), BF16)
    lane = lax.broadcasted_iota(I32, (BLK, HD), 1)
    aug[0] = jnp.where(lane < 3, 1.0, jnp.where(lane == 3, NEG, 0.0)).astype(BF16)
    aug[1] = jnp.where(lane < 3, 1.0, 0.0).astype(BF16)
    qa_ref[...] = qa_in[...]
    acc_ref[...] = acc_in[...]

    total = jnp.int32(0)
    for h in range(GROUP):
        base = (group * GROUP + h) * PICKS
        count = counts[group * GROUP + h]

        def note(j, at, h=h, base=base, count=count):
            todo[3 * at] = h
            todo[3 * at + 1] = lists[base + 2 * j]
            more = 2 * j + 1 < count
            todo[3 * at + 2] = jnp.where(more, lists[base + 2 * j + jnp.where(more, 1, 0)], spare)
            return at + 1

        total = lax.fori_loop(0, (count + 1) >> 1, note, total)
    for n in range(AT_ONCE - 1):
        todo[3 * (total + n)] = n
        todo[3 * (total + n) + 1] = spare
        todo[3 * (total + n) + 2] = spare
    steps = (total + AT_ONCE - 1) // AT_ONCE
    for copy in copies:
        copy.wait()

    def entries(i):
        first = 3 * AT_ONCE * i
        return [tuple(todo[first + 3 * n + k] for k in range(3)) for n in range(AT_ONCE)]

    def scores(h, one, two):
        keys = jnp.concatenate([kv[one, :, :HD], kv[two, :, :HD]], axis=0)
        real = [jnp.where(slot == spare, 0, 1) for slot in (one, two)]
        more = jnp.concatenate([aug[real[0]], aug[real[1]]], axis=0)
        return dot_f32(qa_ref[h], jnp.concatenate([keys, more], axis=1), ((1,), (1,)))

    ones = jnp.ones((2 * BLK, HD), BF16)

    def accumulate():
        def step(i, high):
            work = entries(i)
            for h, one, two in work:
                s = scores(h, one, two) * C2
                values = jnp.concatenate([kv[one, :, HD:], kv[two, :, HD:]], axis=0)
                acc_ref[h] += dot_f32(
                    jnp.exp2(s).astype(BF16), jnp.concatenate([values, ones], axis=1), ((1,), (0,))
                )
                high = jnp.maximum(high, jnp.max(s.reshape(-1, 8, 2 * BLK), axis=0))
            return high

        return jnp.max(lax.fori_loop(0, steps, step, jnp.zeros((8, 2 * BLK), F32)))

    highest = accumulate()

    @pl.when(highest > LIMIT)
    def _():
        rows = qa_ref.shape[1]
        for h in range(GROUP):

            def step(n, gain, h=h):
                mine = todo[3 * n] == h
                s = scores(todo[3 * n], todo[3 * n + 1], todo[3 * n + 2])
                top = jnp.max(s, axis=1, keepdims=True)
                return jnp.maximum(gain, jnp.where(mine, top, 0.0))

            gain = lax.fori_loop(0, total, step, jnp.zeros((rows, 1), F32))
            parts = qa_ref[h, :, HD:].astype(F32)
            old = -(parts[:, 0:1] + parts[:, 1:2] + parts[:, 2:3])
            new = old + gain
            qa_ref[h, :, HD:] = extra_columns(new)
            acc_ref[h] = acc_in[h] * jnp.exp2((old - new) * C2)
        accumulate()

    if final:
        core = scal[0]
        for out, first in ((other_ref, (1 - core) * 2 * BLK), (mine_ref, core * 2 * BLK)):
            rows = pl.ds(pl.multiple_of(first, BLK), 2 * BLK)
            for h in range(GROUP):
                both = acc_ref[h, rows, :]
                out[:, h * HD : (h + 1) * HD] = (both[:, :HD] / both[:, HD:]).astype(BF16)


def crossed_kernel(right, left, out_ref):
    out_ref[...] = jnp.zeros_like(out_ref)


def weight_tiles(scal, w_ref, w_buf, sem, sibling, rel_tiles):
    core, me = scal[0], scal[2]
    rows, cols = w_buf.shape[1:]
    first = jnp.where(core == (1 if sibling else 0), 0, rows)
    copies = []
    for n, tile in enumerate(rel_tiles):
        step = (2, 1, 3, 0)[tile // 2]
        col = ((me + step) % 4) * (2 * cols) + (tile % 2) * cols
        copies.append(
            pltpu.make_async_copy(
                w_ref.at[pl.ds(pl.multiple_of(first, rows), rows), pl.ds(pl.multiple_of(col, cols), cols)],
                w_buf.at[n],
                sem.at[n],
            )
        )
    for copy in copies:
        copy.start()
    return copies


def part_kernel(sibling, tiles, scal, ctx, w_ref, out_ref, w_buf, sem):
    copies = weight_tiles(scal, w_ref, w_buf, sem, sibling, tiles)
    for n, copy in enumerate(copies):
        copy.wait()
        out_ref[n] = dot_f32(ctx[...], w_buf[n], ((1,), (0,)))


def add_part_kernel(sibling, tiles, scal, ctx, part, w_ref, *rest):
    outs, (w_buf, sem) = rest[: len(tiles)], rest[len(tiles) :]
    copies = weight_tiles(scal, w_ref, w_buf, sem, sibling, tiles)
    for n, copy in enumerate(copies):
        copy.wait()
        outs[n][...] = (part[n] + dot_f32(ctx[...], w_buf[n], ((1,), (0,)))).astype(outs[n].dtype)


def both_parts_kernel(tiles, scal, ctx, ctx_sib, w_ref, *rest):
    outs, (w_own, w_sib, sem_own, sem_sib) = rest[: len(tiles)], rest[len(tiles) :]
    own = weight_tiles(scal, w_ref, w_own, sem_own, False, tiles)
    sib = weight_tiles(scal, w_ref, w_sib, sem_sib, True, tiles)
    for n in range(len(tiles)):
        own[n].wait()
        part = dot_f32(ctx[...], w_own[n], ((1,), (0,)))
        sib[n].wait()
        outs[n][...] = (part + dot_f32(ctx_sib[...], w_sib[n], ((1,), (0,)))).astype(outs[n].dtype)


def spec(space):
    return pl.BlockSpec(memory_space=space)


def call(
    kernel, name, outs, args, spaces, scratch=(), out_spaces=None, flops=0, moved=0, vmem_bytes=VMEM_BYTES
):
    return pl.pallas_call(
        kernel,
        out_shape=outs,
        in_specs=[spec(s) for s in spaces],
        out_specs=[spec(s) for s in (out_spaces or [pltpu.VMEM] * len(outs))],
        scratch_shapes=list(scratch),
        compiler_params=pltpu.CompilerParams(vmem_limit_bytes=vmem_bytes),
        cost_estimate=pl.CostEstimate(flops=flops, bytes_accessed=moved, transcendentals=0),
        name=name,
    )(*args)


def shape(dims, dtype):
    return jax.ShapeDtypeStruct(dims, dtype)


def local(queries, key_states, value_states, vert_blocks, window_size, slash_offsets, out_weight):
    smem, vmem, anywhere = pltpu.SMEM, pltpu.VMEM, pl.ANY
    place = lax.axis_index("seq").astype(I32)
    me = lax.axis_index("tp").astype(I32)
    core = place % 2
    scal = jnp.stack([core, place, me])
    block = shape((1, BLK, 2 * HD), BF16)

    k_sib = swap_cores(key_states)
    v_sib = swap_cores(value_states)
    q_sib = swap_cores(queries)
    unit, tail = call(
        pick_kernel, "pick", [shape((2, BLK, 2 * HD), BF16), shape((BLK, 2 * HD), BF16)],
        (scal, vert_blocks, key_states, value_states, k_sib, v_sib),
        [smem] + [anywhere] * 5,
        [
            pltpu.VMEM((4,) + key_states.shape, BF16),
            pltpu.SMEM(vert_blocks.shape, I32),
            pltpu.SemaphoreType.DMA((5,)),
        ],
        moved=1_000_000,
        vmem_bytes=60 * 1024 * 1024,
    )

    halo = lax.ppermute(tail, "seq", [(i, i + 2) for i in range(2 * NX * NZ - 2)])

    up1, up2, down1 = up(unit, 0), up(unit, 0, 2), down(unit, (1,))
    opposite = along_x(unit, 2, 0)
    up2, halo = lax.optimization_barrier((up2, halo))
    up3 = up(jnp.concatenate([up2, opposite], axis=0), 0)
    down2 = down(jnp.concatenate([down1, opposite], axis=0), (2, 1))
    down3 = down(down2, (3, 2))
    first = jnp.concatenate([unit, up1, up2, down1], axis=0)
    right1, left1 = along_x(first, 1, 0), along_x(first, -1, 0)

    rows = 2 * queries.shape[0]
    wide = (GROUP, rows, 2 * HD)
    qa, acc, lists, counts = call(
        local_kernel,
        "near_part",
        [shape(wide, BF16), shape(wide, F32), shape((16 * PICKS,), I32), shape((16,), I32)],
        (
            scal, vert_blocks, window_size, slash_offsets, jnp.asarray(slot_table()), queries, q_sib, key_states, k_sib, value_states, v_sib, halo,
        ),
        [smem] * 5 + [anywhere] * 7,
        [
            pltpu.VMEM((2,) + queries.shape, BF16),
            pltpu.VMEM((4,) + key_states.shape, BF16),
            pltpu.VMEM((BLK, 2 * HD), BF16),
            pltpu.VMEM((GROUP, rows, HD), BF16),
            pltpu.VMEM((rows + BLK, HD), BF16),
            pltpu.VMEM((rows + BLK, HD), BF16),
            pltpu.SMEM((GROUP * 8,), I32),
            pltpu.SemaphoreType.DMA((7,)),
        ],
        [vmem, vmem, smem, smem],
        flops=5_000_000_000,
        moved=100_000,
    )

    def far(n, pieces, qa, acc):
        sizes = [p.shape[0] for p in pieces]
        scratch = [
            pltpu.VMEM((sum(sizes) + 1, BLK, 2 * HD), BF16),
            pltpu.VMEM((2, BLK, HD), BF16),
            pltpu.SMEM((3 * (GROUP * PICKS + AT_ONCE),), I32),
            pltpu.SemaphoreType.DMA((len(sizes),)),
        ]
        final = n == 1
        outs = [shape(wide, BF16), shape(wide, F32)]
        if final:
            scratch = [pltpu.VMEM(wide, BF16), pltpu.VMEM(wide, F32)] + scratch
            outs = [shape((rows // 2, GROUP * HD), BF16)] * 2
        return call(
            functools.partial(far_kernel, n, sizes, final),
            "far_part",
            outs,
            (scal, lists, counts, qa, acc, *pieces),
            [smem] * 3 + [vmem] * 2 + [anywhere] * len(sizes),
            scratch,
            flops=6_000_000_000,
            moved=100_000,
        )

    up4 = up(up3, 1)
    second = jnp.concatenate([up3[:2], up4[:2], down2[:2], down3[:2]], axis=0)
    crossed = call(
        crossed_kernel, "crossed", [shape((8, HD), F32)], (right1, left1), [anywhere] * 2,
        flops=6_000_000_000,
    )[0]
    second, acc, crossed = lax.optimization_barrier((second, acc, crossed))
    right2, left2 = along_x(second, 1, 3), along_x(second, -1, 3)
    qa, acc = far(0, [first, right1, left1, opposite, up3, up4, down2, down3], qa, acc)
    up5, up6 = up(up4[2:], 2), up(up4[2:], 2, 2)
    down4 = down(down3[2:], (3,))
    ctx_mine, ctx_other = far(1, [right2, left2, up5, up6, down4], qa, acc)
    ctx_sib = swap_cores(ctx_other)

    half_rows, half = rows // 2, out_weight.shape[1] // 8
    depth = GROUP * HD

    def w_scratch(count):
        return [pltpu.VMEM((count, depth, half), BF16)], [pltpu.SemaphoreType.DMA((count,))]

    tile_bf, tile_f = shape((half_rows, half), BF16), shape((half_rows, half), F32)

    def own_part(tiles):
        return call(
            functools.partial(part_kernel, False, tiles), "own_part",
            [shape((len(tiles), half_rows, half), F32)],
            (scal, ctx_mine, out_weight), [smem, vmem, anywhere],
            sum(w_scratch(len(tiles)), []), flops=1_000_000, moved=1_000,
        )[0]

    def sib_part(tiles, part):
        return call(
            functools.partial(add_part_kernel, True, tiles), "sib_part", [tile_bf] * 2,
            (scal, ctx_sib, part, out_weight), [smem, vmem, vmem, anywhere],
            sum(w_scratch(2), []), flops=1_000_000, moved=1_000,
        )

    opp0, opp1 = sib_part((0, 1), own_part((0, 1)))
    via_before = tp_shift(opp0, 1)
    via_after = tp_shift(opp1, -1)

    def both(tiles, out):
        bufs, sems = w_scratch(len(tiles))
        return call(
            functools.partial(both_parts_kernel, tiles), "both_parts", [out] * len(tiles),
            (scal, ctx_mine, ctx_sib, out_weight), [smem, vmem, vmem, anywhere],
            bufs * 2 + sems * 2, flops=1_000_000, moved=1_000,
        )

    after1, before0 = both((3, 4), tile_bf)
    direct1 = tp_shift(after1, 1)
    direct0 = tp_shift(before0, -1)
    after0, before1 = both((2, 5), tile_f)
    own0, own1 = both((6, 7), tile_f)
    summed0 = tp_shift((after0 + via_before.astype(F32)).astype(BF16), 1)
    summed1 = tp_shift((before1 + via_after.astype(F32)).astype(BF16), -1)
    return jnp.concatenate(
        [
            own0 + direct0.astype(F32) + summed0.astype(F32),
            own1 + direct1.astype(F32) + summed1.astype(F32),
        ],
        axis=1,
    ).astype(BF16)


def solution(mesh):
    return jax.shard_map(
        local,
        mesh=mesh,
        in_specs=(
            P("seq", "tp"),
            P("seq", "tp"),
            P("seq", "tp"),
            P("tp", None),
            P("tp"),
            P("tp", None),
            P("tp", None),
        ),
        out_specs=P("seq", "tp"),
        check_vma=False,
    )
```
